128 devices in a mesh: segment: 8 (over x, core), dp: 16 (over z, y).
Axes of the slice: x: 4, y: 4, z: 4, core: 2. Of those that a mesh axis runs over, the one named last changes fastest.
Arguments:
- embeds: bfloat16 [2, 16, 128, 4096], P(None, 'dp'), may hold values from -6 to 6
- base_weight: bfloat16 [8, 4096, 4096], P('segment', 'dp'), may hold values from -0.09375 to 0.09375
- norm_gain: float32 [8, 4096], P('segment'), may hold values from 0.25 to 1.75
- skill_down: bfloat16 [8, 16, 8, 4096], P('segment'), may hold values from -0.09375 to 0.09375
- skill_up: bfloat16 [8, 16, 8, 4096], P('segment'), may hold values from -2 to 2
- task_ids: int32 [2, 16], replicated, may hold values from 0 to 1835
- allocation: int32 [1836, 16], replicated, may hold values 0 or 1
- target_lengths: int32 [2, 16], replicated, may hold values from 1 to 128
- cotangent: bfloat16 [2, 16, 128, 4096], P(None, 'dp'), may hold values from -6 to 6
Outputs:
- hidden: bfloat16 [8, 2, 16, 128, 4096], P('segment', None, 'dp')
- input_grads: bfloat16 [8, 2, 16, 128, 4096], P('segment', None, 'dp')
- grad_down: float32 [8, 16, 8, 4096], P('segment', None, None, 'dp')
- grad_up: float32 [8, 16, 8, 4096], P('segment', None, None, 'dp')
The draws below stay inside these ranges and needn't reach their ends.
All inputs are finite; a program needn't handle non-finite values.
Results may differ from the reference program's by a relative error of at most 0.019.
Values may be sent and summed in bfloat16 or wider, within the bound.
A program may use at most 192 MiB of HBM per device.

```python
import jax
import jax.numpy as jnp
from jax import lax

D = 4096
SKILLS = 16
RANK = 8
TASKS = 1836
MICRO = 2
ROWS = 128
N_SEGMENT = 8
N_DP = 16


def with_ends(drawn, key, least, high):
    index_at = [jax.random.randint(jax.random.fold_in(key, axis), (), 0, length) for axis, length in enumerate(drawn.shape)]
    main_axis = drawn.shape.index(max(drawn.shape))
    next_to = index_at[:main_axis] + [(index_at[main_axis] + 1) % drawn.shape[main_axis]] + index_at[main_axis + 1:]
    return drawn.at[tuple(index_at)].set(least).at[tuple(next_to)].set(high)


def levels(stream_key, extent, pieces, least, top_value):
    factor_of = 1.0
    for position, parts in pieces:
        heights = jax.random.uniform(jax.random.fold_in(jax.random.fold_in(stream_key, 6), position), (parts,), jnp.float32, least / len(pieces), top_value / len(pieces))
        factor_of = factor_of * jnp.repeat(jnp.exp(heights), extent[position] // parts).reshape((-1,) + (1,) * (len(extent) - 1 - position))
    return factor_of


def gaussian(stream_key, dims, spread, reach, shards=(), held_as=jnp.bfloat16):
    factor_of = levels(stream_key, dims, shards, -0.22, 0.18) if shards else 1.0
    array = jax.random.normal(stream_key, dims, jnp.float32) * spread * factor_of
    return jnp.minimum(jnp.maximum(array, -reach), reach).astype(held_as)


def setup_inputs(seed: int = 0) -> dict:
    keys = jax.random.split(jax.random.key(seed), 10)
    embeds = gaussian(keys[0], (MICRO, N_DP, ROWS, D), 1.0, 6.0, ((1, 16),))
    base_weight = gaussian(keys[1], (N_SEGMENT, D, D), D ** -0.5, 0.09375, ((0, 8), (1, 16)))
    norm_gain = jnp.clip(1.0 + 0.15 * jax.random.normal(keys[2], (N_SEGMENT, D), jnp.float32), 0.25, 1.75)
    skill_down = gaussian(keys[3], (N_SEGMENT, SKILLS, RANK, D), D ** -0.5, 0.09375, ((0, 8),))
    skill_up = gaussian(keys[4], (N_SEGMENT, SKILLS, RANK, D), RANK ** -0.5, 2.0, ((0, 8),))
    task_ids = with_ends(jax.random.randint(keys[5], (MICRO, N_DP), 0, TASKS), jax.random.fold_in(keys[5], 1), 0, TASKS - 1).astype(jnp.int32)
    allocation = with_ends((jax.random.randint(keys[6], (TASKS, SKILLS), 0, 2) < 1).astype(jnp.int32), jax.random.fold_in(keys[6], 1), 0, 1)
    target_lengths = with_ends(jax.random.randint(keys[7], (MICRO, N_DP), 1, ROWS + 1), jax.random.fold_in(keys[7], 1), 1, ROWS).astype(jnp.int32)
    cotangent = gaussian(keys[8], (MICRO, N_DP, ROWS, D), 1.0, 6.0, ((1, 16),))
    return {"embeds": embeds, "base_weight": base_weight, "norm_gain": norm_gain, "skill_down": skill_down, "skill_up": skill_up, "task_ids": task_ids, "allocation": allocation, "target_lengths": target_lengths, "cotangent": cotangent}


EPS = 1e-06

def mixing_table(task_ids, allocation):
    onehot = (task_ids[..., None] == jnp.arange(TASKS, dtype=jnp.int32)).astype(jnp.float32)
    alloc = allocation.astype(jnp.float32)
    counts = jnp.maximum(lax.optimization_barrier(jnp.sum(alloc, axis=1, keepdims=True)), 1.0)
    return jnp.einsum('...t,ts->...s', onehot, alloc / counts, precision=lax.Precision.HIGHEST)

def prepare(x, gain, down_t):
    xf = x.astype(jnp.float32)
    inv = lax.rsqrt(lax.optimization_barrier(jnp.mean(xf * xf, axis=-1, keepdims=True)) + EPS)
    normed = (xf * inv * gain).astype(jnp.bfloat16)
    low = jnp.dot(normed, down_t.T, preferred_element_type=jnp.float32).astype(jnp.bfloat16)
    return (normed, low, inv)

def forward_one(x, weight, gain, down_t, up_t):
    normed, low, inv = prepare(x, gain, down_t)
    total = x.astype(jnp.float32) + jnp.dot(normed, weight, preferred_element_type=jnp.float32)
    total = total + jnp.dot(low, up_t, preferred_element_type=jnp.float32)
    return total.astype(jnp.bfloat16)

def backward_core(x, normed, low, inv, grad_out, weight, gain, down_t, up_t):
    g_low = jnp.dot(grad_out, up_t.T, preferred_element_type=jnp.float32).astype(jnp.bfloat16)
    dnorm = jnp.dot(grad_out, weight.T, preferred_element_type=jnp.float32)
    dnorm = dnorm + jnp.dot(g_low, down_t, preferred_element_type=jnp.float32)
    seq_down = jnp.dot(g_low.T, normed, preferred_element_type=jnp.float32)
    seq_up = jnp.dot(low.T, grad_out, preferred_element_type=jnp.float32)
    xf = x.astype(jnp.float32)
    scaled = gain * dnorm
    grad_in = grad_out.astype(jnp.float32) + inv * scaled - xf * inv * inv * inv * lax.optimization_barrier(jnp.mean(xf * scaled, axis=-1, keepdims=True))
    return (grad_in.astype(jnp.bfloat16), seq_down, seq_up)

def backward_one(x, grad_out, weight, gain, down_t, up_t):
    normed, low, inv = prepare(x, gain, down_t)
    return backward_core(x, normed, low, inv, grad_out, weight, gain, down_t, up_t)

def reference(embeds, base_weight, norm_gain, skill_down, skill_up, task_ids, allocation, target_lengths, cotangent):
    mix = mixing_table(task_ids, allocation)
    flat_mix = mix.reshape(MICRO * N_DP, SKILLS)
    state = embeds.reshape(MICRO * N_DP, ROWS, D)
    downs, ups, inputs, outputs = ([], [], [], [])
    for level in range(N_SEGMENT):
        down_t = jnp.einsum('qs,srd->qrd', flat_mix, skill_down[level].astype(jnp.float32), precision=lax.Precision.HIGHEST).astype(jnp.bfloat16)
        up_t = jnp.einsum('qs,srd->qrd', flat_mix, skill_up[level].astype(jnp.float32), precision=lax.Precision.HIGHEST).astype(jnp.bfloat16)
        downs.append(down_t)
        ups.append(up_t)
        inputs.append(state)
        state = jax.vmap(forward_one, in_axes=(0, None, None, 0, 0))(state, base_weight[level], norm_gain[level], down_t, up_t)
        outputs.append(state)
    mask = jnp.arange(ROWS, dtype=jnp.int32)[None, None, :] < target_lengths[..., None]
    grad_state = (cotangent * mask[..., None].astype(jnp.bfloat16)).reshape(MICRO * N_DP, ROWS, D)
    grads_in = [None] * N_SEGMENT
    grads_down = [None] * N_SEGMENT
    grads_up = [None] * N_SEGMENT
    for level in reversed(range(N_SEGMENT)):
        grad_state, seq_down, seq_up = jax.vmap(backward_one, in_axes=(0, 0, None, None, 0, 0))(inputs[level], grad_state, base_weight[level], norm_gain[level], downs[level], ups[level])
        grads_in[level] = grad_state
        part_down = jnp.einsum('mjs,mjrd->jsrd', mix, seq_down.reshape(MICRO, N_DP, RANK, D), precision=lax.Precision.HIGHEST)
        part_up = jnp.einsum('mjs,mjrd->jsrd', mix, seq_up.reshape(MICRO, N_DP, RANK, D), precision=lax.Precision.HIGHEST)
        grads_down[level] = lax.optimization_barrier(jnp.sum(part_down.astype(jnp.bfloat16).astype(jnp.float32), axis=0))
        grads_up[level] = lax.optimization_barrier(jnp.sum(part_up.astype(jnp.bfloat16).astype(jnp.float32), axis=0))
    hidden = jnp.stack(outputs).reshape(N_SEGMENT, MICRO, N_DP, ROWS, D)
    input_grads = jnp.stack(grads_in).reshape(N_SEGMENT, MICRO, N_DP, ROWS, D)
    return (hidden, input_grads, jnp.stack(grads_down), jnp.stack(grads_up))
```

```python
import functools

import jax
import jax.numpy as jnp
from jax import lax
from jax.experimental import pallas as pl
from jax.experimental.pallas import tpu as pltpu
from jax.sharding import PartitionSpec as P

EPS = 1e-06
MESH = pl.DeviceIdType.MESH
SIDE = 4
CHUNKS = 4
F32 = jnp.float32
BF16 = jnp.bfloat16


def dot(a, b, dims=((1,), (0,))):
    return lax.dot_general(a, b, (dims, ((), ())), preferred_element_type=F32)


def kernel(
    emb, w, gain, sdown, sup, tasks, alloc, lens, cot,
    hidden, grads_in, gdown, gup,
    wbuf, xbuf, obuf, hbuf, gbuf, gout, down, up, lowbuf, invbuf, mixb, mixrow, seq, got,
    first_s, first_r, second_s, second_r, own_sem,
    x_s, x_r, g_s, g_r, load_sem, store_sem, seq_s, seq_r,
):
    segments = lax.axis_size("segment")
    members = lax.axis_size("dp")
    seg = lax.axis_index("segment")
    me = lax.axis_index("dp")
    micro, rows, width = emb.shape
    block = w.shape[0]
    half = width // 2
    part = block // 2
    skills, rank = sdown.shape[0], sdown.shape[1]
    z, y = me // SIDE, lax.rem(me, SIDE)
    last = segments - 1

    barrier = pltpu.get_barrier_semaphore()

    def greet(d, c):
        pl.semaphore_signal(barrier, inc=1, device_id=(seg, lax.rem(me + d, members)), device_id_type=MESH)
        return c

    lax.fori_loop(1, members, greet, 0)
    for d in (1, segments - 1):
        pl.semaphore_signal(barrier, inc=1, device_id=(lax.rem(seg + d, segments), me), device_id_type=MESH)
    pl.semaphore_wait(barrier, members + 1)

    def at(h, df, ds):
        dy, dz = (df, ds) if h == 0 else (ds, df)
        return lax.rem(z + dz + SIDE, SIDE) * SIDE + lax.rem(y + dy + SIDE, SIDE)

    def rows_of(h, df, ds, sub=None):
        start = at(h, df, ds) * block
        if sub is None:
            return wbuf.at[h, pl.ds(pl.multiple_of(start, block), block), :]
        return wbuf.at[h, pl.ds(pl.multiple_of(start + sub * part, part), part), :]

    def send(src, dst, s, r, to):
        c = pltpu.make_async_remote_copy(
            src_ref=src, dst_ref=dst, send_sem=s, recv_sem=r, device_id=(seg, to), device_id_type=MESH
        )
        c.start()
        return c

    sent = []
    first = [[None] * 4 for _ in range(2)]
    second = [[[None] * 4 for _ in range(4)] for _ in range(2)]
    order = (0, -1, 1, 2)
    own = []
    for h in range(2):
        mine = w.at[:, h * half : (h + 1) * half]
        for d, way in enumerate((1, -1)):
            first[h][d] = send(mine, rows_of(h, 0, 0), first_s.at[h, d], first_r.at[h, d], at(h, way, 0))
    for h in range(2):
        mine = w.at[:, h * half : (h + 1) * half]
        for d, way in enumerate((1, -1)):
            second[h][0][d] = send(mine, rows_of(h, 0, 0), second_s.at[h, 0, d], second_r.at[h, 0, d], at(h, 0, way))
    for h in range(2):
        c = pltpu.make_async_copy(w.at[:, h * half : (h + 1) * half], rows_of(h, 0, 0), own_sem.at[h])
        c.start()
        own.append(c)

    @pl.when(seg == 0)
    def _():
        pltpu.make_async_copy(emb, xbuf, load_sem.at[0]).start()

    @pl.when(seg == last)
    def _():
        pltpu.make_async_copy(cot, gbuf, load_sem.at[1]).start()

    table = alloc[...].astype(F32).astype(BF16)
    total = alloc.shape[0]
    picked = (tasks[...] == lax.broadcasted_iota(jnp.int32, (tasks.shape[0], total), 1)).astype(F32).astype(BF16)
    uses = dot(picked, table)
    mix = uses / jnp.maximum(jnp.sum(uses, axis=1, keepdims=True), 1.0)
    for s in range(skills):
        mixb[s] = jnp.broadcast_to(mix[:, s : s + 1], mixb.shape[1:])
    step = mixb.shape[2]

    def adapters(i, c):
        cols = pl.ds(pl.multiple_of(i * step, step), step)
        for m in range(micro):
            for source, target in ((sdown, down), (sup, up)):
                acc = jnp.zeros((rank, step), F32)
                for s in range(skills):
                    acc = acc + mixb[s, pl.ds(m * members + me, 1), :] * source[s, :, cols].astype(F32)
                target[m, :, cols] = acc.astype(BF16)
        return c

    lax.fori_loop(0, width // step, adapters, 0)

    def arrived_first(h):
        for d, way in enumerate((1, -1)):
            first[h][d].wait_recv()
            src = rows_of(h, -way, 0, d)
            first[h][2 + d] = send(src, src, first_s.at[h, 2 + d], first_r.at[h, 2 + d], at(h, way, 0))

    def spread(h, i):
        for d, way in enumerate((1, -1)):
            src = rows_of(h, order[i], 0)
            second[h][i][d] = send(src, src, second_s.at[h, i, d], second_r.at[h, i, d], at(h, 0, way))

    def pass_on(h, i):
        for d, way in enumerate((1, -1)):
            second[h][i][d].wait_recv()
            src = rows_of(h, order[i], -way, d)
            second[h][i][2 + d] = send(src, src, second_s.at[h, i, 2 + d], second_r.at[h, i, 2 + d], at(h, 0, way))

    for h in range(2):
        arrived_first(h)
    for h in range(2):
        spread(h, 1)
        spread(h, 2)
    for h in range(2):
        pass_on(h, 0)
    for h in range(2):
        first[h][2].wait_recv()
        first[h][3].wait_recv()
        spread(h, 3)
    for i in (1, 2, 3):
        for h in range(2):
            pass_on(h, i)
    for h in range(2):
        own[h].wait()
        for i in range(4):
            second[h][i][2].wait_recv()
            second[h][i][3].wait_recv()
    for h in range(2):
        for d in range(4):
            first[h][d].wait_send()
            for i in range(4):
                second[h][i][d].wait_send()

    wide = width // CHUNKS
    tile = 512

    def hop(buf, target, m, q, s, r, to):
        cols = pl.ds(q * wide, wide)
        return pltpu.make_async_remote_copy(
            src_ref=buf.at[m, :, cols], dst_ref=target.at[m, :, cols], send_sem=s.at[m, q], recv_sem=r.at[m, q],
            device_id=(to, me), device_id_type=MESH,
        )

    onward = functools.partial(hop, obuf, xbuf, s=x_s, r=x_r, to=lax.rem(seg + 1, segments))
    back = functools.partial(hop, gout, gbuf, s=g_s, r=g_r, to=lax.rem(seg + last, segments))

    @pl.when(seg == 0)
    def _():
        pltpu.make_async_copy(emb, xbuf, load_sem.at[0]).wait()

    for m in range(micro):

        @pl.when(seg > 0)
        def _():
            for q in range(CHUNKS):
                onward(m, q).wait_recv()

        def squares(i, acc):
            v = xbuf[m, :, pl.ds(pl.multiple_of(i * tile, tile), tile)].astype(F32)
            return acc + jnp.sum(v * v, axis=1, keepdims=True)

        ss = lax.fori_loop(0, width // tile, squares, jnp.zeros((rows, 1), F32))
        inv = lax.rsqrt(ss / width + EPS)
        invbuf[m] = inv

        def normed(i, c):
            cols = pl.ds(pl.multiple_of(i * tile, tile), tile)
            hbuf[m, :, cols] = (xbuf[m, :, cols].astype(F32) * inv * gain[:, cols]).astype(BF16)
            return c

        lax.fori_loop(0, width // tile, normed, 0)
        low = dot(hbuf[m], down[m], ((1,), (1,))).astype(BF16)
        lowbuf[m] = low
        for q in range(CHUNKS):

            def forward(i, c):
                at_col = q * wide + i * tile
                cols = pl.ds(pl.multiple_of(at_col, tile), tile)
                inner = pl.ds(pl.multiple_of(at_col - (q * wide // half) * half, tile), tile)
                acc = dot(hbuf[m], wbuf[q * wide // half, :, inner])
                acc = acc + dot(low, up[m, :, cols])
                obuf[m, :, cols] = (xbuf[m, :, cols].astype(F32) + acc).astype(BF16)
                return c

            lax.fori_loop(0, wide // tile, forward, 0)

            @pl.when(seg < last)
            def _():
                onward(m, q).start()

        pltpu.make_async_copy(obuf.at[m], hidden.at[m], store_sem.at[m]).start()

    @pl.when(seg == last)
    def _():
        pltpu.make_async_copy(cot, gbuf, load_sem.at[1]).wait()
        for m in range(micro):
            keep = lax.broadcasted_iota(jnp.int32, (rows, tile), 0) < lens[m, me]

            def masked(i, c):
                cols = pl.ds(pl.multiple_of(i * tile, tile), tile)
                gbuf[m, :, cols] = jnp.where(keep, gbuf[m, :, cols].astype(F32), 0.0).astype(BF16)
                return c

            lax.fori_loop(0, width // tile, masked, 0)

    btile = 256
    for m in range(micro):

        @pl.when(seg < last)
        def _():
            for q in range(CHUNKS):
                back(m, q).wait_recv()

        glow = dot(gbuf[m], up[m], ((1,), (1,))).astype(BF16)
        inv = invbuf[m]

        def along(i, acc):
            cols = pl.ds(pl.multiple_of(i * tile, tile), tile)
            step_out = obuf[m, :, cols].astype(F32) - xbuf[m, :, cols].astype(F32)
            return acc + jnp.sum(gbuf[m, :, cols].astype(F32) * step_out, axis=1, keepdims=True)

        coef = lax.fori_loop(0, width // tile, along, jnp.zeros((rows, 1), F32)) / width * inv * inv
        for q in range(CHUNKS):

            def backward(i, c):
                cols = pl.ds(pl.multiple_of(q * wide + i * btile, btile), btile)
                dh = dot(gbuf[m, :, :half], wbuf[0, cols, :], ((1,), (1,)))
                dh = dh + dot(gbuf[m, :, half:], wbuf[1, cols, :], ((1,), (1,)))
                dh = dh + dot(glow, down[m, :, cols])
                out = gbuf[m, :, cols].astype(F32) + inv * (gain[:, cols] * dh) - xbuf[m, :, cols].astype(F32) * coef
                gout[m, :, cols] = out.astype(BF16)
                return c

            lax.fori_loop(0, wide // btile, backward, 0)

            @pl.when(seg > 0)
            def _():
                back(m, q).start()

        pltpu.make_async_copy(gout.at[m], grads_in.at[m], store_sem.at[micro + m]).start()

        def adapter_grads(i, c):
            cols = pl.ds(pl.multiple_of(i * tile, tile), tile)
            seq[m, :, cols] = dot(glow, hbuf[m, :, cols], ((0,), (0,)))
            seq[micro + m, :, cols] = dot(lowbuf[m], gbuf[m, :, cols], ((0,), (0,)))
            return c

        lax.fori_loop(0, width // tile, adapter_grads, 0)

    def share(d):
        to = lax.rem(me + d, members)
        return pltpu.make_async_remote_copy(
            src_ref=seq.at[:, :, pl.ds(pl.multiple_of(to * block, block), block)], dst_ref=got.at[d],
            send_sem=seq_s.at[d], recv_sem=seq_r.at[d], device_id=(seg, to), device_id_type=MESH,
        )

    def share_start(d, c):
        share(d).start()
        return c

    def add(mine, source, fresh):
        for t, target in enumerate((gdown, gup)):
            for s in range(skills):
                p = sum(mixb[s, pl.ds(m * members + source, 1), :] * mine[t * micro + m] for m in range(micro))
                p = p.astype(BF16).astype(F32)
                target[s] = p if fresh else target[s] + p

    lax.fori_loop(1, members, share_start, 0)
    own_cols = pl.ds(pl.multiple_of(me * block, block), block)
    add([seq[i, :, own_cols] for i in range(2 * micro)], me, True)

    def take(d, c):
        share(d).wait_recv()
        add([got[d, i] for i in range(2 * micro)], lax.rem(me - d + members, members), False)
        return c

    lax.fori_loop(1, members, take, 0)

    def drain(d, c):
        share(d).wait_send()
        return c

    lax.fori_loop(1, members, drain, 0)
    for m in range(micro):
        pltpu.make_async_copy(obuf.at[m], hidden.at[m], store_sem.at[m]).wait()
        pltpu.make_async_copy(gout.at[m], grads_in.at[m], store_sem.at[micro + m]).wait()

    @pl.when(seg < last)
    def _():
        for m in range(micro):
            for q in range(CHUNKS):
                onward(m, q).wait_send()

    @pl.when(seg > 0)
    def _():
        for m in range(micro):
            for q in range(CHUNKS):
                back(m, q).wait_send()


def shards(embeds, base_weight, norm_gain, skill_down, skill_up, task_ids, allocation, target_lengths, cotangent):
    micro, _, rows, width = embeds.shape
    block = base_weight.shape[1]
    _, skills, rank, _ = skill_down.shape
    members = lax.axis_size("dp")
    anywhere = pl.BlockSpec(memory_space=pl.ANY)
    vmem = pl.BlockSpec(memory_space=pltpu.VMEM)
    smem = pl.BlockSpec(memory_space=pltpu.SMEM)
    stream = jax.ShapeDtypeStruct((micro, rows, width), BF16)
    grad = jax.ShapeDtypeStruct((skills, rank, block), F32)
    dma = pltpu.SemaphoreType.DMA
    held = pltpu.VMEM((micro, rows, width), BF16)
    hidden, grads_in, gdown, gup = pl.pallas_call(
        kernel,
        out_shape=(stream, stream, grad, grad),
        in_specs=[anywhere, anywhere, vmem, vmem, vmem, vmem, vmem, smem, anywhere],
        out_specs=(anywhere, anywhere, vmem, vmem),
        scratch_shapes=[
            pltpu.VMEM((2, width, width // 2), BF16),
            held, held, held, held, held,
            pltpu.VMEM((micro, rank, width), BF16),
            pltpu.VMEM((micro, rank, width), BF16),
            pltpu.VMEM((micro, rows, rank), BF16),
            pltpu.VMEM((micro, rows, 1), F32),
            pltpu.VMEM((skills, micro * members, block), F32),
            pltpu.VMEM((8, 128), F32),
            pltpu.VMEM((2 * micro, rank, width), F32),
            pltpu.VMEM((members, 2 * micro, rank, block), F32),
            dma((2, 4)), dma((2, 4)), dma((2, 4, 4)), dma((2, 4, 4)), dma((2,)),
            dma((micro, CHUNKS)), dma((micro, CHUNKS)), dma((micro, CHUNKS)), dma((micro, CHUNKS)),
            dma((2,)), dma((2 * micro,)), dma((members,)), dma((members,)),
        ],
        compiler_params=pltpu.CompilerParams(
            collective_id=0, has_side_effects=True, vmem_limit_bytes=60 * 1024 * 1024
        ),
    )(
        embeds[:, 0], base_weight[0], norm_gain, skill_down[0], skill_up[0],
        task_ids.reshape(-1, 1), allocation, target_lengths, cotangent[:, 0],
    )
    return (hidden[None, :, None], grads_in[None, :, None], gdown[None], gup[None])


def solution(mesh):
    in_specs = (
        P(None, "dp", None, None),
        P("segment", "dp", None),
        P("segment", None),
        P("segment", None, None, None),
        P("segment", None, None, None),
        P(),
        P(),
        P(),
        P(None, "dp", None, None),
    )
    out_specs = (
        P("segment", None, "dp", None, None),
        P("segment", None, "dp", None, None),
        P("segment", None, None, "dp"),
        P("segment", None, None, "dp"),
    )
    return jax.shard_map(shards, mesh=mesh, in_specs=in_specs, out_specs=out_specs, check_vma=False)
```

```python
import functools

import jax
import jax.numpy as jnp
from jax import lax
from jax.experimental import pallas as pl
from jax.experimental.pallas import tpu as pltpu
from jax.sharding import PartitionSpec as P

EPS = 1e-06
MESH = pl.DeviceIdType.MESH
SIDE = 4
CHUNKS = 4
F32 = jnp.float32
BF16 = jnp.bfloat16


def dot(a, b, dims=((1,), (0,))):
    return lax.dot_general(a, b, (dims, ((), ())), preferred_element_type=F32)


def kernel(
    emb, w, gain, sdown, sup, tasks, alloc, lens, cot,
    hidden, grads_in, gdown, gup,
    wbuf, xbuf, obuf, hbuf, gbuf, gout, down, up, lowbuf, invbuf, mixb, table, acc, seq, got,
    first_s, first_r, second_s, second_r, own_sem,
    x_s, x_r, g_s, g_r, load_sem, store_sem, seq_s, seq_r,
):
    segments = lax.axis_size("segment")
    members = lax.axis_size("dp")
    seg = lax.axis_index("segment")
    me = lax.axis_index("dp")
    micro, rows, width = emb.shape
    block = w.shape[0]
    half = width // 2
    part = block // 2
    skills, rank = sdown.shape[0], sdown.shape[1]
    z, y = me // SIDE, lax.rem(me, SIDE)
    last = segments - 1

    barrier = pltpu.get_barrier_semaphore()

    def greet(d, c):
        pl.semaphore_signal(barrier, inc=1, device_id=(seg, lax.rem(me + d, members)), device_id_type=MESH)
        return c

    lax.fori_loop(1, members, greet, 0)
    for d in (1, segments - 1):
        pl.semaphore_signal(barrier, inc=1, device_id=(lax.rem(seg + d, segments), me), device_id_type=MESH)
    pl.semaphore_wait(barrier, members + 1)

    def at(h, df, ds):
        dy, dz = (df, ds) if h == 0 else (ds, df)
        return lax.rem(z + dz + SIDE, SIDE) * SIDE + lax.rem(y + dy + SIDE, SIDE)

    def rows_of(h, df, ds, sub=None):
        start = at(h, df, ds) * block
        if sub is None:
            return wbuf.at[h, pl.ds(pl.multiple_of(start, block), block), :]
        return wbuf.at[h, pl.ds(pl.multiple_of(start + sub * part, part), part), :]

    def send(src, dst, s, r, to):
        c = pltpu.make_async_remote_copy(
            src_ref=src, dst_ref=dst, send_sem=s, recv_sem=r, device_id=(seg, to), device_id_type=MESH
        )
        c.start()
        return c

    sent = []
    first = [[None] * 4 for _ in range(2)]
    second = [[[None] * 4 for _ in range(4)] for _ in range(2)]
    order = (0, -1, 1, 2)
    own = []
    for h in range(2):
        mine = w.at[:, h * half : (h + 1) * half]
        for d, way in enumerate((1, -1)):
            first[h][d] = send(mine, rows_of(h, 0, 0), first_s.at[h, d], first_r.at[h, d], at(h, way, 0))
    for h in range(2):
        mine = w.at[:, h * half : (h + 1) * half]
        for d, way in enumerate((1, -1)):
            second[h][0][d] = send(mine, rows_of(h, 0, 0), second_s.at[h, 0, d], second_r.at[h, 0, d], at(h, 0, way))
    for h in range(2):
        c = pltpu.make_async_copy(w.at[:, h * half : (h + 1) * half], rows_of(h, 0, 0), own_sem.at[h])
        c.start()
        own.append(c)

    pltpu.make_async_copy(alloc, table, load_sem.at[2]).start()

    @pl.when(seg == 0)
    def _():
        pltpu.make_async_copy(emb, xbuf, load_sem.at[0]).start()

    @pl.when(seg == last)
    def _():
        pltpu.make_async_copy(cot, gbuf, load_sem.at[1]).start()

    pltpu.make_async_copy(alloc, table, load_sem.at[2]).wait()
    known = table[...].astype(F32).astype(BF16)
    for m in range(micro):
        picked = lax.broadcasted_iota(jnp.int32, (table.shape[0], members), 0) == tasks[m : m + 1, :]
        uses = dot(picked.astype(F32).astype(BF16), known, ((0,), (0,)))
        mix = uses / jnp.maximum(jnp.sum(uses, axis=1, keepdims=True), 1.0)
        for s in range(skills):
            mixb[s, m * members : (m + 1) * members] = jnp.broadcast_to(mix[:, s : s + 1], (members, mixb.shape[2]))
    step = mixb.shape[2]

    def adapters(i, c):
        cols = pl.ds(pl.multiple_of(i * step, step), step)
        for m in range(micro):
            for source, target in ((sdown, down), (sup, up)):
                acc = jnp.zeros((rank, step), F32)
                for s in range(skills):
                    acc = acc + mixb[s, pl.ds(m * members + me, 1), :] * source[s, :, cols].astype(F32)
                target[m, :, cols] = acc.astype(BF16)
        return c

    lax.fori_loop(0, width // step, adapters, 0)

    def arrived_first(h):
        for d, way in enumerate((1, -1)):
            first[h][d].wait_recv()
            src = rows_of(h, -way, 0, d)
            first[h][2 + d] = send(src, src, first_s.at[h, 2 + d], first_r.at[h, 2 + d], at(h, way, 0))

    def spread(h, i):
        for d, way in enumerate((1, -1)):
            src = rows_of(h, order[i], 0)
            second[h][i][d] = send(src, src, second_s.at[h, i, d], second_r.at[h, i, d], at(h, 0, way))

    def pass_on(h, i):
        for d, way in enumerate((1, -1)):
            second[h][i][d].wait_recv()
            src = rows_of(h, order[i], -way, d)
            second[h][i][2 + d] = send(src, src, second_s.at[h, i, 2 + d], second_r.at[h, i, 2 + d], at(h, 0, way))

    for h in range(2):
        arrived_first(h)
    for h in range(2):
        spread(h, 1)
        spread(h, 2)
    for h in range(2):
        pass_on(h, 0)
    for h in range(2):
        first[h][2].wait_recv()
        first[h][3].wait_recv()
        spread(h, 3)
    for i in (1, 2, 3):
        for h in range(2):
            pass_on(h, i)
    for h in range(2):
        own[h].wait()
        for i in range(4):
            second[h][i][2].wait_recv()
            second[h][i][3].wait_recv()
    for h in range(2):
        for d in range(4):
            first[h][d].wait_send()
            for i in range(4):
                second[h][i][d].wait_send()

    wide = width // CHUNKS

    def chunk(q):
        return pl.ds(pl.multiple_of(q * wide, wide), wide)

    def by_columns(q):
        return wbuf[q // (CHUNKS // 2), :, chunk(lax.rem(q, CHUNKS // 2))]

    def hop(buf, target, m, q, s, r, to):
        return pltpu.make_async_remote_copy(
            src_ref=buf.at[m, :, chunk(q)], dst_ref=target.at[m, :, chunk(q)], send_sem=s.at[m, q], recv_sem=r.at[m, q],
            device_id=(to, me), device_id_type=MESH,
        )

    onward = functools.partial(hop, obuf, xbuf, s=x_s, r=x_r, to=lax.rem(seg + 1, segments))
    back = functools.partial(hop, gout, gbuf, s=g_s, r=g_r, to=lax.rem(seg + last, segments))
    column = jnp.zeros((rows, 1), F32)
    narrow = jnp.zeros((rows, rank), F32)

    def share(d):
        to = lax.rem(me + d, members)
        return pltpu.make_async_remote_copy(
            src_ref=seq.at[:, :, pl.ds(pl.multiple_of(to * block, block), block)], dst_ref=got.at[d],
            send_sem=seq_s.at[d], recv_sem=seq_r.at[d], device_id=(seg, to), device_id_type=MESH,
        )

    def share_start(d, c):
        share(d).start()
        return c

    def over_chunks(body, init=0):
        return lax.fori_loop(0, CHUNKS, body, init)

    def forward(m, as_it_comes):
        if as_it_comes:
            acc[...] = jnp.zeros_like(acc)

        def take_in(q, c):
            ss, lw = c

            @pl.when(seg > 0)
            def _():
                onward(m, q).wait_recv()

            v = xbuf[m, :, chunk(q)].astype(F32)
            h = (v * gain[:, chunk(q)]).astype(BF16)
            if as_it_comes:
                for i in range(2):
                    acc[:, i * half : (i + 1) * half] += dot(h, wbuf[i, chunk(q), :])
            else:
                hbuf[m, :, chunk(q)] = h
            return ss + jnp.sum(v * v, axis=1, keepdims=True), lw + dot(h, down[m, :, chunk(q)], ((1,), (1,)))

        ss, lw = over_chunks(take_in, (column, narrow))
        inv = lax.rsqrt(ss / width + EPS)
        low = (lw * inv).astype(BF16)
        invbuf[m] = inv
        lowbuf[m] = low

        def give_out(q, c):
            total = acc[:, chunk(q)] if as_it_comes else dot(hbuf[m], by_columns(q))
            total = xbuf[m, :, chunk(q)].astype(F32) + inv * total + dot(low, up[m, :, chunk(q)])
            obuf[m, :, chunk(q)] = total.astype(BF16)

            @pl.when(seg < last)
            def _():
                onward(m, q).start()

            return c

        over_chunks(give_out)
        pltpu.make_async_copy(obuf.at[m], hidden.at[m], store_sem.at[m]).start()

    def normed(m):
        def body(q, c):
            h = xbuf[m, :, chunk(q)].astype(F32) * invbuf[m] * gain[:, chunk(q)]
            hbuf[m, :, chunk(q)] = h.astype(BF16)
            return c

        over_chunks(body)

    def backward(m, kind):
        if kind == "comes":
            acc[...] = jnp.zeros_like(acc)

        def take_in(q, c):
            along, gl = c

            @pl.when(seg < last)
            def _():
                back(m, q).wait_recv()

            g = gbuf[m, :, chunk(q)]
            if kind == "comes":
                for i in range(2):
                    acc[:, i * half : (i + 1) * half] += dot(g, wbuf[i, chunk(q), :])
            change = obuf[m, :, chunk(q)].astype(F32) - xbuf[m, :, chunk(q)].astype(F32)
            along = along + jnp.sum(g.astype(F32) * change, axis=1, keepdims=True)
            return along, gl + dot(g, up[m, :, chunk(q)], ((1,), (1,)))

        along, gl = over_chunks(take_in, (column, narrow))
        glow = gl.astype(BF16)
        inv = invbuf[m]
        coef = along / width * inv * inv

        def adapter_grads():
            def body(q, c):
                seq[m, :, chunk(q)] = dot(glow, hbuf[m, :, chunk(q)], ((0,), (0,)))
                seq[micro + m, :, chunk(q)] = dot(lowbuf[m], gbuf[m, :, chunk(q)], ((0,), (0,)))
                return c

            over_chunks(body)

            @pl.when(m == micro - 1)
            def _():
                lax.fori_loop(1, members, share_start, 0)

        @pl.when(seg == 0)
        def _():
            adapter_grads()

        def give_out(q, c):
            if kind == "comes":
                dh = acc[:, chunk(q)]
            elif kind == "columns":
                dh = dot(gbuf[m], by_columns(q))
            else:
                dh = dot(gbuf[m, :, :half], wbuf[0, chunk(q), :], ((1,), (1,)))
                dh = dh + dot(gbuf[m, :, half:], wbuf[1, chunk(q), :], ((1,), (1,)))
            dh = dh + dot(glow, down[m, :, chunk(q)])
            out = gbuf[m, :, chunk(q)].astype(F32) + inv * (gain[:, chunk(q)] * dh)
            gout[m, :, chunk(q)] = (out - xbuf[m, :, chunk(q)].astype(F32) * coef).astype(BF16)

            @pl.when(seg > 0)
            def _():
                back(m, q).start()

            return c

        over_chunks(give_out)
        pltpu.make_async_copy(gout.at[m], grads_in.at[m], store_sem.at[micro + m]).start()

        @pl.when(seg > 0)
        def _():
            adapter_grads()

    def each_micro(body):
        def step(m, c):
            body(m)
            return c

        lax.fori_loop(0, micro, step, 0)

    even = lax.rem(seg, 2) == 0

    @pl.when(seg == 0)
    def _():
        pltpu.make_async_copy(emb, xbuf, load_sem.at[0]).wait()

    @pl.when(even)
    def _():
        each_micro(lambda m: forward(m, True))

    @pl.when(jnp.logical_not(even) & (seg < last))
    def _():
        each_micro(lambda m: forward(m, False))

    @pl.when(seg < last)
    def _():
        each_micro(normed)

        size = 512
        count = width // size

        def place(i, j):
            inner = lax.rem(j, count // 2)
            return wbuf.at[
                j // (count // 2), pl.ds(pl.multiple_of(i * size, size), size), pl.ds(pl.multiple_of(inner * size, size), size)
            ]

        def turn(i, c):
            def inner(j, c):
                a, b = place(i, j)[...].T, place(j, i)[...].T
                place(j, i)[...] = a
                place(i, j)[...] = b
                return c

            return lax.fori_loop(i, count, inner, c)

        lax.fori_loop(0, count, turn, 0)

    @pl.when(even)
    def _():
        each_micro(lambda m: backward(m, "columns"))

    @pl.when(jnp.logical_not(even) & (seg < last))
    def _():
        each_micro(lambda m: backward(m, "comes"))

    @pl.when(seg == last)
    def _():
        pltpu.make_async_copy(cot, gbuf, load_sem.at[1]).wait()

        def both(m):
            keep = lax.broadcasted_iota(jnp.int32, (rows, wide), 0) < lens[m, me]

            def masked(q, c):
                gbuf[m, :, chunk(q)] = jnp.where(keep, gbuf[m, :, chunk(q)].astype(F32), 0.0).astype(BF16)
                return c

            over_chunks(masked)
            forward(m, False)
            normed(m)
            backward(m, "rows")

        each_micro(both)

    def add(mine, source, fresh):
        for t, target in enumerate((gdown, gup)):
            for s in range(skills):
                p = sum(mixb[s, pl.ds(m * members + source, 1), :] * mine[t * micro + m] for m in range(micro))
                p = p.astype(BF16).astype(F32)
                target[s] = p if fresh else target[s] + p

    own_cols = pl.ds(pl.multiple_of(me * block, block), block)
    add([seq[i, :, own_cols] for i in range(2 * micro)], me, True)

    def take(d, c):
        share(d).wait_recv()
        add([got[d, i] for i in range(2 * micro)], lax.rem(me - d + members, members), False)
        return c

    lax.fori_loop(1, members, take, 0)

    def drain(d, c):
        share(d).wait_send()
        return c

    lax.fori_loop(1, members, drain, 0)
    for m in range(micro):
        pltpu.make_async_copy(obuf.at[m], hidden.at[m], store_sem.at[m]).wait()
        pltpu.make_async_copy(gout.at[m], grads_in.at[m], store_sem.at[micro + m]).wait()

    @pl.when(seg < last)
    def _():
        for m in range(micro):
            for q in range(CHUNKS):
                onward(m, q).wait_send()

    @pl.when(seg > 0)
    def _():
        for m in range(micro):
            for q in range(CHUNKS):
                back(m, q).wait_send()


def shards(embeds, base_weight, norm_gain, skill_down, skill_up, task_ids, allocation, target_lengths, cotangent):
    micro, _, rows, width = embeds.shape
    block = base_weight.shape[1]
    _, skills, rank, _ = skill_down.shape
    members = lax.axis_size("dp")
    anywhere = pl.BlockSpec(memory_space=pl.ANY)
    vmem = pl.BlockSpec(memory_space=pltpu.VMEM)
    smem = pl.BlockSpec(memory_space=pltpu.SMEM)
    stream = jax.ShapeDtypeStruct((micro, rows, width), BF16)
    grad = jax.ShapeDtypeStruct((skills, rank, block), F32)
    dma = pltpu.SemaphoreType.DMA
    held = pltpu.VMEM((micro, rows, width), BF16)
    hidden, grads_in, gdown, gup = pl.pallas_call(
        kernel,
        out_shape=(stream, stream, grad, grad),
        in_specs=[anywhere, anywhere, vmem, vmem, vmem, vmem, anywhere, smem, anywhere],
        out_specs=(anywhere, anywhere, vmem, vmem),
        scratch_shapes=[
            pltpu.VMEM((2, width, width // 2), BF16),
            held, held, held, held, held,
            pltpu.VMEM((micro, rank, width), BF16),
            pltpu.VMEM((micro, rank, width), BF16),
            pltpu.VMEM((micro, rows, rank), BF16),
            pltpu.VMEM((micro, rows, 1), F32),
            pltpu.VMEM((skills, micro * members, block), F32),
            pltpu.VMEM(allocation.shape, jnp.int32),
            pltpu.VMEM((rows, width), F32),
            pltpu.VMEM((2 * micro, rank, width), F32),
            pltpu.VMEM((members, 2 * micro, rank, block), F32),
            dma((2, 4)), dma((2, 4)), dma((2, 4, 4)), dma((2, 4, 4)), dma((2,)),
            dma((micro, CHUNKS)), dma((micro, CHUNKS)), dma((micro, CHUNKS)), dma((micro, CHUNKS)),
            dma((3,)), dma((2 * micro,)), dma((members,)), dma((members,)),
        ],
        compiler_params=pltpu.CompilerParams(
            collective_id=0, has_side_effects=True, vmem_limit_bytes=60 * 1024 * 1024
        ),
    )(
        embeds[:, 0], base_weight[0], norm_gain, skill_down[0], skill_up[0],
        task_ids, allocation, target_lengths, cotangent[:, 0],
    )
    return (hidden[None, :, None], grads_in[None, :, None], gdown[None], gup[None])


def solution(mesh):
    in_specs = (
        P(None, "dp", None, None),
        P("segment", "dp", None),
        P("segment", None),
        P("segment", None, None, None),
        P("segment", None, None, None),
        P(),
        P(),
        P(),
        P(None, "dp", None, None),
    )
    out_specs = (
        P("segment", None, "dp", None, None),
        P("segment", None, "dp", None, None),
        P("segment", None, None, "dp"),
        P("segment", None, None, "dp"),
    )
    return jax.shard_map(shards, mesh=mesh, in_specs=in_specs, out_specs=out_specs, check_vma=False)
```

```python
import functools

import jax
import jax.numpy as jnp
from jax import lax
from jax.experimental import pallas as pl
from jax.experimental.pallas import tpu as pltpu
from jax.sharding import PartitionSpec as P

EPS = 1e-06
MESH = pl.DeviceIdType.MESH
SIDE = 4
CHUNKS = 8
F32 = jnp.float32
BF16 = jnp.bfloat16


def dot(a, b, dims=((1,), (0,))):
    return lax.dot_general(a, b, (dims, ((), ())), preferred_element_type=F32)


def kernel(
    emb, w, gain, sdown, sup, tasks, alloc, lens, cot,
    hidden, grads_in, gdown, gup,
    wbuf, vis, xbuf, obuf, hbuf, gbuf, gout, down, up, lowbuf, glowbuf, invbuf, mixb, table, acc, seq, got,
    *sems,
):
    main_sems, rest_sems, visit_sems = sems[:4], sems[4:8], sems[8:12]
    over_s, over_r, back_s, back_r, own_sem = sems[12:17]
    x_s, x_r, g_s, g_r, load_sem, store_sem, seq_s, seq_r = sems[17:]
    segments = lax.axis_size("segment")
    members = lax.axis_size("dp")
    seg = lax.axis_index("segment")
    me = lax.axis_index("dp")
    micro, rows, width = emb.shape
    block = w.shape[0]
    half = width // 2
    part = block // 2
    skills, rank = sdown.shape[0], sdown.shape[1]
    z, y = me // SIDE, lax.rem(me, SIDE)
    last = segments - 1

    barrier = pltpu.get_barrier_semaphore()

    def greet(d, c):
        pl.semaphore_signal(barrier, inc=1, device_id=(seg, lax.rem(me + d, members)), device_id_type=MESH)
        return c

    lax.fori_loop(1, members, greet, 0)
    for d in (1, 2, segments - 2, segments - 1):
        pl.semaphore_signal(barrier, inc=1, device_id=(lax.rem(seg + d, segments), me), device_id_type=MESH)
    pl.semaphore_wait(barrier, members + 3)

    wide = width // CHUNKS

    def chunk(q):
        return pl.ds(pl.multiple_of(q * wide, wide), wide)

    def by_columns(q):
        return wbuf[q // (CHUNKS // 2), :, chunk(lax.rem(q, CHUNKS // 2))]

    def hop(buf, target, m, q, s, r, to):
        return pltpu.make_async_remote_copy(
            src_ref=buf.at[m, :, chunk(q)], dst_ref=target.at[m, :, chunk(q)], send_sem=s.at[m, q], recv_sem=r.at[m, q],
            device_id=(to, me), device_id_type=MESH,
        )

    onward = functools.partial(hop, obuf, xbuf, s=x_s, r=x_r, to=lax.rem(seg + 1, segments))
    back = functools.partial(hop, gout, gbuf, s=g_s, r=g_r, to=lax.rem(seg + last, segments))
    column = jnp.zeros((rows, 1), F32)
    narrow = jnp.zeros((rows, rank), F32)

    def share(d):
        to = lax.rem(me + d, members)
        return pltpu.make_async_remote_copy(
            src_ref=seq.at[:, :, pl.ds(pl.multiple_of(to * block, block), block)], dst_ref=got.at[d],
            send_sem=seq_s.at[d], recv_sem=seq_r.at[d], device_id=(seg, to), device_id_type=MESH,
        )

    def share_start(d, c):
        share(d).start()
        return c

    def over_chunks(body, init=0):
        return lax.fori_loop(0, CHUNKS, body, init)

    def each_micro(body):
        def step(m, c):
            body(m)
            return c

        lax.fori_loop(0, micro, step, 0)

    def begin(m, kind):
        if kind == "comes":
            acc[m] = jnp.zeros((rows, width), F32)

        def take_in(q, c):
            ss, lw = c
            if kind != "early":

                @pl.when(seg > 0)
                def _():
                    onward(m, q).wait_recv()

            v = xbuf[m, :, chunk(q)].astype(F32)
            h = (v * gain[:, chunk(q)]).astype(BF16)
            if kind == "comes":
                for i in range(2):
                    acc[m, :, i * half : (i + 1) * half] += dot(h, wbuf[i, chunk(q), :])
            else:
                hbuf[m, :, chunk(q)] = h
            return ss + jnp.sum(v * v, axis=1, keepdims=True), lw + dot(h, down[m, :, chunk(q)], ((1,), (1,)))

        ss, lw = over_chunks(take_in, (column, narrow))
        inv = lax.rsqrt(ss / width + EPS)
        invbuf[m] = inv
        lowbuf[m] = (lw * inv).astype(BF16)

    def finish(m, kind):
        inv = invbuf[m]
        low = lowbuf[m]

        def give_out(q, c):
            total = dot(hbuf[m], by_columns(q)) if kind == "columns" else acc[m, :, chunk(q)]
            total = xbuf[m, :, chunk(q)].astype(F32) + inv * total + dot(low, up[m, :, chunk(q)])
            obuf[m, :, chunk(q)] = total.astype(BF16)

            @pl.when(seg < last)
            def _():
                onward(m, q).start()

            return c

        over_chunks(give_out)
        pltpu.make_async_copy(obuf.at[m], hidden.at[m], store_sem.at[m]).start()

    def forward(m, kind):
        begin(m, kind)
        finish(m, kind)

    extra = vis.shape[2]
    most = half - extra
    order = (0, -1, 1, 2)
    ways = (1, -1)
    opening = seg < 2
    closing = seg >= segments - 2

    def at(h, df, ds):
        dy, dz = (df, ds) if h == 0 else (ds, df)
        return lax.rem(z + dz + SIDE, SIDE) * SIDE + lax.rem(y + dy + SIDE, SIDE)

    def block_of(buf, cols, h, df, ds, sub=None):
        start = at(h, df, ds) * block
        if sub is None:
            return buf.at[h, pl.ds(pl.multiple_of(start, block), block), cols]
        return buf.at[h, pl.ds(pl.multiple_of(start + sub * part, part), part), cols]

    def remote(src, dst, s, r, to, to_seg=seg):
        return pltpu.make_async_remote_copy(
            src_ref=src, dst_ref=dst, send_sem=s, recv_sem=r, device_id=(to_seg, to), device_id_type=MESH
        )

    class Stream:
        def __init__(self, buf, cols, mine, f_s, f_r, s_s, s_r):
            self.ref = functools.partial(block_of, buf, cols)
            self.mine, self.sems = mine, (f_s, f_r, s_s, s_r)

        def first(self, h, d):
            way = ways[d % 2]
            dst = self.ref(h, 0, 0) if d < 2 else self.ref(h, -way, 0, d - 2)
            src = self.mine(h) if d < 2 else dst
            return remote(src, dst, self.sems[0].at[h, d], self.sems[1].at[h, d], at(h, way, 0))

        def second(self, h, i, d):
            way = ways[d % 2]
            dst = self.ref(h, order[i], 0) if d < 2 else self.ref(h, order[i], -way, d - 2)
            src = self.mine(h) if d < 2 and i == 0 else dst
            return remote(src, dst, self.sems[2].at[h, i, d], self.sems[3].at[h, i, d], at(h, 0, way))

        def open(self):
            for h in range(2):
                for d in range(2):
                    self.first(h, d).start()
            for h in range(2):
                self.spread(h, 0)

        def arrived_first(self, h):
            for d in range(2):
                self.first(h, d).wait_recv()
                self.first(h, 2 + d).start()

        def spread(self, h, i):
            for d in range(2):
                self.second(h, i, d).start()

        def pass_on(self, h, i):
            for d in range(2):
                self.second(h, i, d).wait_recv()
                self.second(h, i, 2 + d).start()

        def first_done(self, h):
            for d in range(2):
                self.first(h, 2 + d).wait_recv()

        def second_done(self, h, i):
            for d in range(2):
                self.second(h, i, 2 + d).wait_recv()

        def sent(self):
            for h in range(2):
                for d in range(4):
                    self.first(h, d).wait_send()
                    for i in range(4):
                        self.second(h, i, d).wait_send()

    side = pl.ds(most, extra)
    main = Stream(wbuf, pl.ds(0, most), lambda h: w.at[:, pl.ds(h * half, most)], *main_sems)
    rest = Stream(wbuf, side, lambda h: w.at[:, pl.ds(h * half + most, extra)], *rest_sems)
    visit = Stream(vis, pl.ds(0, extra), lambda h: block_of(vis, pl.ds(0, extra), h, 0, 0), *visit_sems)

    def go_over(h):
        return remote(
            w.at[:, pl.ds(h * half + most, extra)], block_of(vis, pl.ds(0, extra), h, 0, 0),
            over_s.at[h], over_r.at[h], me, lax.rem(seg + segments - 2, segments),
        )

    def come_back(h, i, j):
        return remote(
            block_of(vis, pl.ds(0, extra), h, order[i], order[j]), block_of(wbuf, side, h, order[i], order[j]),
            back_s.at[h, i * 4 + j], back_r.at[h, i * 4 + j], me, lax.rem(seg + 2, segments),
        )

    def on_all_but_opening(body):
        pl.when(jnp.logical_not(opening))(body)

    def start_own():
        main.open()
        on_all_but_opening(rest.open)

    @pl.when(opening)
    def _():
        for h in range(2):
            go_over(h).start()

    @pl.when(jnp.logical_not(closing))
    def _():
        start_own()

    own = []
    for h in range(2):
        c = pltpu.make_async_copy(
            w.at[:, h * half : (h + 1) * half], block_of(wbuf, pl.ds(0, half), h, 0, 0), own_sem.at[h]
        )
        c.start()
        own.append(c)
    pltpu.make_async_copy(alloc, table, load_sem.at[2]).start()

    @pl.when(seg == 0)
    def _():
        pltpu.make_async_copy(emb, xbuf, load_sem.at[0]).start()

    @pl.when(seg == last)
    def _():
        pltpu.make_async_copy(cot, gbuf, load_sem.at[1]).start()


    @pl.when(closing)
    def _():
        for h in range(2):
            go_over(h).wait_recv()
        visit.open()
        for h in range(2):
            visit.arrived_first(h)
        for h in range(2):
            visit.spread(h, 1)
            visit.spread(h, 2)
        for h in range(2):
            come_back(h, 1, 0).start()
            come_back(h, 2, 0).start()
            visit.pass_on(h, 0)
        for h in range(2):
            visit.first_done(h)
            visit.spread(h, 3)
        start_own()
        for i in range(4):
            for h in range(2):
                if i > 0:
                    visit.pass_on(h, i)
                come_back(h, i, 1).start()
                come_back(h, i, 2).start()
        for h in range(2):
            come_back(h, 3, 0).start()
        for i in range(4):
            for h in range(2):
                visit.second_done(h, i)
                come_back(h, i, 3).start()

    pltpu.make_async_copy(alloc, table, load_sem.at[2]).wait()
    known = table[...].astype(F32).astype(BF16)
    for m in range(micro):
        picked = lax.broadcasted_iota(jnp.int32, (table.shape[1], members), 0) == tasks[m : m + 1, :]
        uses = dot(picked.astype(F32).astype(BF16), known, ((0,), (1,)))
        mix = uses / jnp.maximum(jnp.sum(uses, axis=1, keepdims=True), 1.0)
        for s in range(skills):
            mixb[s, m * members : (m + 1) * members] = jnp.broadcast_to(mix[:, s : s + 1], (members, mixb.shape[2]))
    step = mixb.shape[2]

    def adapters(i, c):
        cols = pl.ds(pl.multiple_of(i * step, step), step)
        for m in range(micro):
            for source, target in ((sdown, down), (sup, up)):
                acc = jnp.zeros((rank, step), F32)
                for s in range(skills):
                    acc = acc + mixb[s, pl.ds(m * members + me, 1), :] * source[s, :, cols].astype(F32)
                target[m, :, cols] = acc.astype(BF16)
        return c

    lax.fori_loop(0, width // step, adapters, 0)

    @pl.when(seg == 0)
    def _():
        pltpu.make_async_copy(emb, xbuf, load_sem.at[0]).wait()
        each_micro(lambda m: begin(m, "early"))
        acc[...] = jnp.zeros_like(acc)

    def used(df, ds, hs=(0, 1)):
        @pl.when(seg == 0)
        def _():
            for h in hs:
                start = pl.multiple_of(at(h, df, ds) * block, block)
                for m in range(micro):
                    acc[m, :, h * half : h * half + most] += dot(
                        hbuf[m, :, pl.ds(start, block)], wbuf[h, pl.ds(start, block), :most]
                    )

    def everywhere(step, *which):
        getattr(main, step)(*which)
        on_all_but_opening(lambda: getattr(rest, step)(*which))

    for h in range(2):
        everywhere("arrived_first", h)
    for h in range(2):
        everywhere("spread", h, 1)
        everywhere("spread", h, 2)
    for h in range(2):
        own[h].wait()
    used(0, 0)
    used(-1, 0)
    used(1, 0)
    for h in range(2):
        everywhere("pass_on", h, 0)
    for h in range(2):
        everywhere("first_done", h)
        everywhere("spread", h, 3)
    used(2, 0)
    for i in range(4):
        if i > 0:
            for h in range(2):
                everywhere("pass_on", h, i)
        used(order[i], -1)
        used(order[i], 1)

    @pl.when(opening)
    def _():
        for h in range(2):
            for i in range(4):
                for j in range(4):
                    if i + j > 0:
                        come_back(h, i, j).wait_recv()
            go_over(h).wait_send()

    @pl.when(seg == 0)
    def _():
        for h in range(2):
            for m in range(micro):
                acc[m, :, h * half + most : (h + 1) * half] = dot(hbuf[m], wbuf[h, :, most:])

    for i in range(4):
        for h in range(2):
            everywhere("second_done", h, i)
            used(order[i], 2, (h,))

    @pl.when(seg == 0)
    def _():
        each_micro(lambda m: finish(m, "early"))

    everywhere("sent")

    @pl.when(closing)
    def _():
        visit.sent()
        for h in range(2):
            for i in range(4):
                for j in range(4):
                    if i + j > 0:
                        come_back(h, i, j).wait_send()

    def normed(m):
        def body(q, c):
            h = xbuf[m, :, chunk(q)].astype(F32) * invbuf[m] * gain[:, chunk(q)]
            hbuf[m, :, chunk(q)] = h.astype(BF16)
            return c

        over_chunks(body)

    def adapter_grads(m):
        glow = glowbuf[m]

        def body(q, c):
            seq[m, :, chunk(q)] = dot(glow, hbuf[m, :, chunk(q)], ((0,), (0,)))
            seq[micro + m, :, chunk(q)] = dot(lowbuf[m], gbuf[m, :, chunk(q)], ((0,), (0,)))
            return c

        over_chunks(body)

    def share_all():
        lax.fori_loop(1, members, share_start, 0)

    def backward(m, kind, between=None):
        if kind == "comes":
            acc[m] = jnp.zeros((rows, width), F32)

        def take_in(q, c):
            along, gl = c
            if kind != "rows":
                back(m, q).wait_recv()
            g = gbuf[m, :, chunk(q)]
            if kind == "comes":
                for i in range(2):
                    acc[m, :, i * half : (i + 1) * half] += dot(g, wbuf[i, chunk(q), :])
            change = obuf[m, :, chunk(q)].astype(F32) - xbuf[m, :, chunk(q)].astype(F32)
            along = along + jnp.sum(g.astype(F32) * change, axis=1, keepdims=True)
            return along, gl + dot(g, up[m, :, chunk(q)], ((1,), (1,)))

        along, gl = over_chunks(take_in, (column, narrow))
        glow = gl.astype(BF16)
        glowbuf[m] = glow
        inv = invbuf[m]
        coef = along / width * inv * inv
        if between is not None:

            @pl.when(seg == 0)
            def _():
                between(m)

        at_once = 2 if kind == "rows" else 1

        def give_out(q, c):
            cols = pl.ds(pl.multiple_of(q * at_once * wide, at_once * wide), at_once * wide)
            if kind == "comes":
                dh = acc[m, :, cols]
            elif kind == "columns":
                dh = dot(gbuf[m], by_columns(q))
            else:
                turned = dot(wbuf[0, cols, :], gbuf[m, :, :half], ((1,), (1,)))
                turned = turned + dot(wbuf[1, cols, :], gbuf[m, :, half:], ((1,), (1,)))
                dh = turned.T
            dh = dh + dot(glow, down[m, :, cols])
            out = gbuf[m, :, cols].astype(F32) + inv * (gain[:, cols] * dh)
            gout[m, :, cols] = (out - xbuf[m, :, cols].astype(F32) * coef).astype(BF16)

            @pl.when(seg > 0)
            def _():
                for i in range(at_once):
                    back(m, q * at_once + i).start()

            return c

        lax.fori_loop(0, CHUNKS // at_once, give_out, 0)
        pltpu.make_async_copy(gout.at[m], grads_in.at[m], store_sem.at[micro + m]).start()

    even = lax.rem(seg, 2) == 0

    @pl.when(even & (seg > 0))
    def _():
        each_micro(lambda m: forward(m, "comes"))

    @pl.when(jnp.logical_not(even) & (seg < last))
    def _():
        each_micro(lambda m: forward(m, "columns"))

    @pl.when(seg < last)
    def _():
        each_micro(normed)

        size = 512
        count = width // size

        def place(i, j):
            inner = lax.rem(j, count // 2)
            return wbuf.at[
                j // (count // 2), pl.ds(pl.multiple_of(i * size, size), size), pl.ds(pl.multiple_of(inner * size, size), size)
            ]

        def turn(i, c):
            def inner(j, c):
                a, b = place(i, j)[...].T, place(j, i)[...].T
                place(j, i)[...] = a
                place(i, j)[...] = b
                return c

            return lax.fori_loop(i, count, inner, c)

        lax.fori_loop(0, count, turn, 0)

    def before_the_last(m):
        adapter_grads(m)

        @pl.when(m == micro - 1)
        def _():
            share_all()

    @pl.when(even)
    def _():
        each_micro(lambda m: backward(m, "columns", before_the_last))

    @pl.when(jnp.logical_not(even) & (seg < last))
    def _():
        each_micro(lambda m: backward(m, "comes"))

    @pl.when(seg == last)
    def _():
        pltpu.make_async_copy(cot, gbuf, load_sem.at[1]).wait()

        def both(m):
            keep = lax.broadcasted_iota(jnp.int32, (rows, wide), 0) < lens[m, me]

            def masked(q, c):
                gbuf[m, :, chunk(q)] = jnp.where(keep, gbuf[m, :, chunk(q)].astype(F32), 0.0).astype(BF16)
                return c

            over_chunks(masked)
            forward(m, "columns")
            backward(m, "rows")

        each_micro(both)
        each_micro(normed)

    @pl.when(seg > 0)
    def _():
        each_micro(adapter_grads)
        share_all()

    def add(mine, source, fresh):
        for t, target in enumerate((gdown, gup)):
            for s in range(skills):
                p = sum(mixb[s, pl.ds(m * members + source, 1), :] * mine[t * micro + m] for m in range(micro))
                p = p.astype(BF16).astype(F32)
                target[s] = p if fresh else target[s] + p

    own_cols = pl.ds(pl.multiple_of(me * block, block), block)
    add([seq[i, :, own_cols] for i in range(2 * micro)], me, True)

    def take(d, c):
        share(d).wait_recv()
        add([got[d, i] for i in range(2 * micro)], lax.rem(me - d + members, members), False)
        return c

    lax.fori_loop(1, members, take, 0)

    def drain(d, c):
        share(d).wait_send()
        return c

    lax.fori_loop(1, members, drain, 0)
    for m in range(micro):
        pltpu.make_async_copy(obuf.at[m], hidden.at[m], store_sem.at[m]).wait()
        pltpu.make_async_copy(gout.at[m], grads_in.at[m], store_sem.at[micro + m]).wait()

    @pl.when(seg < last)
    def _():
        for m in range(micro):
            for q in range(CHUNKS):
                onward(m, q).wait_send()

    @pl.when(seg > 0)
    def _():
        for m in range(micro):
            for q in range(CHUNKS):
                back(m, q).wait_send()


def shards(embeds, base_weight, norm_gain, skill_down, skill_up, task_ids, allocation, target_lengths, cotangent):
    micro, _, rows, width = embeds.shape
    block = base_weight.shape[1]
    _, skills, rank, _ = skill_down.shape
    members = lax.axis_size("dp")
    anywhere = pl.BlockSpec(memory_space=pl.ANY)
    vmem = pl.BlockSpec(memory_space=pltpu.VMEM)
    smem = pl.BlockSpec(memory_space=pltpu.SMEM)
    stream = jax.ShapeDtypeStruct((micro, rows, width), BF16)
    grad = jax.ShapeDtypeStruct((skills, rank, block), F32)
    dma = pltpu.SemaphoreType.DMA
    held = pltpu.VMEM((micro, rows, width), BF16)
    hidden, grads_in, gdown, gup = pl.pallas_call(
        kernel,
        out_shape=(stream, stream, grad, grad),
        in_specs=[anywhere, anywhere, vmem, vmem, vmem, vmem, anywhere, smem, anywhere],
        out_specs=(anywhere, anywhere, vmem, vmem),
        scratch_shapes=[
            pltpu.VMEM((2, width, width // 2), BF16),
            pltpu.VMEM((2, width, width // 16), BF16),
            held, held, held, held, held,
            pltpu.VMEM((micro, rank, width), BF16),
            pltpu.VMEM((micro, rank, width), BF16),
            pltpu.VMEM((micro, rows, rank), BF16),
            pltpu.VMEM((micro, rows, rank), BF16),
            pltpu.VMEM((micro, rows, 1), F32),
            pltpu.VMEM((skills, micro * members, block), F32),
            pltpu.VMEM(allocation.shape[::-1], jnp.int32),
            pltpu.VMEM((micro, rows, width), F32),
            pltpu.VMEM((2 * micro, rank, width), F32),
            pltpu.VMEM((members, 2 * micro, rank, block), F32),
            *((dma((2, 4)), dma((2, 4)), dma((2, 4, 4)), dma((2, 4, 4))) * 3),
            dma((2,)), dma((2,)), dma((2, 16)), dma((2, 16)), dma((2,)),
            dma((micro, CHUNKS)), dma((micro, CHUNKS)), dma((micro, CHUNKS)), dma((micro, CHUNKS)),
            dma((3,)), dma((2 * micro,)), dma((members,)), dma((members,)),
        ],
        compiler_params=pltpu.CompilerParams(
            collective_id=0, has_side_effects=True, vmem_limit_bytes=60 * 1024 * 1024
        ),
    )(
        embeds[:, 0], base_weight[0], norm_gain, skill_down[0], skill_up[0],
        task_ids, allocation.T, target_lengths, cotangent[:, 0],
    )
    return (hidden[None, :, None], grads_in[None, :, None], gdown[None], gup[None])


def solution(mesh):
    in_specs = (
        P(None, "dp", None, None),
        P("segment", "dp", None),
        P("segment", None),
        P("segment", None, None, None),
        P("segment", None, None, None),
        P(),
        P(),
        P(),
        P(None, "dp", None, None),
    )
    out_specs = (
        P("segment", None, "dp", None, None),
        P("segment", None, "dp", None, None),
        P("segment", None, None, "dp"),
        P("segment", None, None, "dp"),
    )
    return jax.shard_map(shards, mesh=mesh, in_specs=in_specs, out_specs=out_specs, check_vma=False)
```

```python
import functools

import jax
import jax.numpy as jnp
from jax import lax
from jax.experimental import pallas as pl
from jax.experimental.pallas import tpu as pltpu
from jax.sharding import PartitionSpec as P

EPS = 1e-06
MESH = pl.DeviceIdType.MESH
SIDE = 4
CHUNKS = 8
F32 = jnp.float32
BF16 = jnp.bfloat16


def dot(a, b, dims=((1,), (0,))):
    return lax.dot_general(a, b, (dims, ((), ())), preferred_element_type=F32)


def kernel(
    emb, w, gain, sdown, sup, tasks, alloc, lens, cot,
    hidden, grads_in, gdown, gup,
    wbuf, vis, xbuf, obuf, hbuf, gbuf, gout, down, up, lowbuf, glowbuf, invbuf, mixb, table, acc, seq, got,
    *sems,
):
    main_sems, rest_sems, visit_sems = sems[:4], sems[4:8], sems[8:12]
    over_s, over_r, back_s, back_r, own_sem = sems[12:17]
    x_s, x_r, g_s, g_r, load_sem, store_sem, seq_s, seq_r, turn_sem = sems[17:]
    segments = lax.axis_size("segment")
    members = lax.axis_size("dp")
    seg = lax.axis_index("segment")
    me = lax.axis_index("dp")
    micro, rows, width = emb.shape
    block = w.shape[0]
    half = width // 2
    part = block // 2
    skills, rank = sdown.shape[0], sdown.shape[1]
    z, y = me // SIDE, lax.rem(me, SIDE)
    last = segments - 1

    barrier = pltpu.get_barrier_semaphore()

    def greet(d, c):
        pl.semaphore_signal(barrier, inc=1, device_id=(seg, lax.rem(me + d, members)), device_id_type=MESH)
        return c

    lax.fori_loop(1, members, greet, 0)
    for d in (1, 2, segments - 2, segments - 1):
        pl.semaphore_signal(barrier, inc=1, device_id=(lax.rem(seg + d, segments), me), device_id_type=MESH)
    pl.semaphore_wait(barrier, members + 3)

    wide = width // CHUNKS

    def chunk(q):
        return pl.ds(pl.multiple_of(q * wide, wide), wide)

    def by_columns(q):
        return wbuf[q // (CHUNKS // 2), :, chunk(lax.rem(q, CHUNKS // 2))]

    def hop(buf, target, m, q, s, r, to):
        return pltpu.make_async_remote_copy(
            src_ref=buf.at[m, :, chunk(q)], dst_ref=target.at[m, :, chunk(q)], send_sem=s.at[m, q], recv_sem=r.at[m, q],
            device_id=(to, me), device_id_type=MESH,
        )

    onward = functools.partial(hop, obuf, xbuf, s=x_s, r=x_r, to=lax.rem(seg + 1, segments))
    back = functools.partial(hop, gout, gbuf, s=g_s, r=g_r, to=lax.rem(seg + last, segments))
    column = jnp.zeros((rows, 1), F32)
    narrow = jnp.zeros((rows, rank), F32)

    def share(d):
        to = lax.rem(me + d, members)
        return pltpu.make_async_remote_copy(
            src_ref=seq.at[:, :, pl.ds(pl.multiple_of(to * block, block), block)], dst_ref=got.at[d],
            send_sem=seq_s.at[d], recv_sem=seq_r.at[d], device_id=(seg, to), device_id_type=MESH,
        )

    def share_start(d, c):
        share(d).start()
        return c

    def over_chunks(body, init=0):
        return lax.fori_loop(0, CHUNKS, body, init)

    def each_micro(body):
        def step(m, c):
            body(m)
            return c

        lax.fori_loop(0, micro, step, 0)

    def begin(m, kind):
        if kind == "comes":
            acc[m] = jnp.zeros((rows, width), F32)

        def take_in(q, c):
            ss, lw = c
            if kind != "early":

                @pl.when(seg > 0)
                def _():
                    onward(m, q).wait_recv()

            v = xbuf[m, :, chunk(q)].astype(F32)
            h = (v * gain[:, chunk(q)]).astype(BF16)
            if kind == "comes":
                for i in range(2):
                    acc[m, :, i * half : (i + 1) * half] += dot(h, wbuf[i, chunk(q), :])
            else:
                hbuf[m, :, chunk(q)] = h
            return ss + jnp.sum(v * v, axis=1, keepdims=True), lw + dot(h, down[m, :, chunk(q)], ((1,), (1,)))

        ss, lw = over_chunks(take_in, (column, narrow))
        inv = lax.rsqrt(ss / width + EPS)
        invbuf[m] = inv
        lowbuf[m] = (lw * inv).astype(BF16)

    def finish(m, kind):
        inv = invbuf[m]
        low = lowbuf[m]

        def give_out(q, c):
            total = dot(hbuf[m], by_columns(q)) if kind == "columns" else acc[m, :, chunk(q)]
            total = xbuf[m, :, chunk(q)].astype(F32) + inv * total + dot(low, up[m, :, chunk(q)])
            obuf[m, :, chunk(q)] = total.astype(BF16)

            @pl.when(seg < last)
            def _():
                onward(m, q).start()

            return c

        over_chunks(give_out)
        pltpu.make_async_copy(obuf.at[m], hidden.at[m], store_sem.at[m]).start()

    def forward(m, kind):
        begin(m, kind)
        finish(m, kind)

    extra = vis.shape[2]
    most = half - extra
    order = (0, -1, 1, 2)
    ways = (1, -1)
    opening = seg < 2
    closing = seg >= segments - 2

    def at(h, df, ds):
        dy, dz = (df, ds) if h == 0 else (ds, df)
        return lax.rem(z + dz + SIDE, SIDE) * SIDE + lax.rem(y + dy + SIDE, SIDE)

    def block_of(buf, cols, h, df, ds, sub=None):
        start = at(h, df, ds) * block
        if sub is None:
            return buf.at[h, pl.ds(pl.multiple_of(start, block), block), cols]
        return buf.at[h, pl.ds(pl.multiple_of(start + sub * part, part), part), cols]

    def remote(src, dst, s, r, to, to_seg=seg):
        return pltpu.make_async_remote_copy(
            src_ref=src, dst_ref=dst, send_sem=s, recv_sem=r, device_id=(to_seg, to), device_id_type=MESH
        )

    class Stream:
        def __init__(self, buf, cols, mine, f_s, f_r, s_s, s_r):
            self.ref = functools.partial(block_of, buf, cols)
            self.mine, self.sems = mine, (f_s, f_r, s_s, s_r)

        def first(self, h, d):
            way = ways[d % 2]
            dst = self.ref(h, 0, 0) if d < 2 else self.ref(h, -way, 0, d - 2)
            src = self.mine(h) if d < 2 else dst
            return remote(src, dst, self.sems[0].at[h, d], self.sems[1].at[h, d], at(h, way, 0))

        def second(self, h, i, d):
            way = ways[d % 2]
            dst = self.ref(h, order[i], 0) if d < 2 else self.ref(h, order[i], -way, d - 2)
            src = self.mine(h) if d < 2 and i == 0 else dst
            return remote(src, dst, self.sems[2].at[h, i, d], self.sems[3].at[h, i, d], at(h, 0, way))

        def open(self):
            for h in range(2):
                for d in range(2):
                    self.first(h, d).start()
            for h in range(2):
                self.spread(h, 0)

        def arrived_first(self, h):
            for d in range(2):
                self.first(h, d).wait_recv()
                self.first(h, 2 + d).start()

        def spread(self, h, i):
            for d in range(2):
                self.second(h, i, d).start()

        def pass_on(self, h, i):
            for d in range(2):
                self.second(h, i, d).wait_recv()
                self.second(h, i, 2 + d).start()

        def first_done(self, h):
            for d in range(2):
                self.first(h, 2 + d).wait_recv()

        def second_done(self, h, i):
            for d in range(2):
                self.second(h, i, 2 + d).wait_recv()

        def sent(self):
            for h in range(2):
                for d in range(4):
                    self.first(h, d).wait_send()
                    for i in range(4):
                        self.second(h, i, d).wait_send()

    side = pl.ds(most, extra)
    main = Stream(wbuf, pl.ds(0, most), lambda h: w.at[:, pl.ds(h * half, most)], *main_sems)
    rest = Stream(wbuf, side, lambda h: w.at[:, pl.ds(h * half + most, extra)], *rest_sems)
    visit = Stream(vis, pl.ds(0, extra), lambda h: block_of(vis, pl.ds(0, extra), h, 0, 0), *visit_sems)

    def go_over(h):
        return remote(
            w.at[:, pl.ds(h * half + most, extra)], block_of(vis, pl.ds(0, extra), h, 0, 0),
            over_s.at[h], over_r.at[h], me, lax.rem(seg + segments - 2, segments),
        )

    def come_back(h, i, j):
        return remote(
            block_of(vis, pl.ds(0, extra), h, order[i], order[j]), block_of(wbuf, side, h, order[i], order[j]),
            back_s.at[h, i * 4 + j], back_r.at[h, i * 4 + j], me, lax.rem(seg + 2, segments),
        )

    def on_all_but_opening(body):
        pl.when(jnp.logical_not(opening))(body)

    def start_own():
        main.open()
        on_all_but_opening(rest.open)

    @pl.when(opening)
    def _():
        for h in range(2):
            go_over(h).start()

    shared = seg >= 2
    later = shared & (lax.rem(seg, 2) == 1)

    @pl.when(jnp.logical_not(closing) & jnp.logical_not(later))
    def _():
        start_own()

    own = []
    for h in range(2):
        c = pltpu.make_async_copy(
            w.at[:, h * half : (h + 1) * half], block_of(wbuf, pl.ds(0, half), h, 0, 0), own_sem.at[h]
        )
        c.start()
        own.append(c)
    pltpu.make_async_copy(alloc, table, load_sem.at[2]).start()

    @pl.when(seg == 0)
    def _():
        pltpu.make_async_copy(emb, xbuf, load_sem.at[0]).start()

    @pl.when(seg == last)
    def _():
        pltpu.make_async_copy(cot, gbuf, load_sem.at[1]).start()


    @pl.when(closing)
    def _():
        for h in range(2):
            go_over(h).wait_recv()
        visit.open()
        pl.when(jnp.logical_not(later))(start_own)
        for h in range(2):
            visit.arrived_first(h)
        for h in range(2):
            visit.spread(h, 1)
            visit.spread(h, 2)
        for h in range(2):
            come_back(h, 1, 0).start()
            come_back(h, 2, 0).start()
            visit.pass_on(h, 0)
        for h in range(2):
            visit.first_done(h)
            visit.spread(h, 3)
        for i in range(4):
            for h in range(2):
                if i > 0:
                    visit.pass_on(h, i)
                come_back(h, i, 1).start()
                come_back(h, i, 2).start()
        for h in range(2):
            come_back(h, 3, 0).start()
        for i in range(4):
            for h in range(2):
                visit.second_done(h, i)
                come_back(h, i, 3).start()

    pltpu.make_async_copy(alloc, table, load_sem.at[2]).wait()
    known = table[...].astype(F32).astype(BF16)
    for m in range(micro):
        picked = lax.broadcasted_iota(jnp.int32, (table.shape[1], members), 0) == tasks[m : m + 1, :]
        uses = dot(picked.astype(F32).astype(BF16), known, ((0,), (1,)))
        mix = uses / jnp.maximum(jnp.sum(uses, axis=1, keepdims=True), 1.0)
        for s in range(skills):
            mixb[s, m * members : (m + 1) * members] = jnp.broadcast_to(mix[:, s : s + 1], (members, mixb.shape[2]))
    step = mixb.shape[2]

    def adapters(i, c):
        cols = pl.ds(pl.multiple_of(i * step, step), step)
        for m in range(micro):
            for source, target in ((sdown, down), (sup, up)):
                acc = jnp.zeros((rank, step), F32)
                for s in range(skills):
                    acc = acc + mixb[s, pl.ds(m * members + me, 1), :] * source[s, :, cols].astype(F32)
                target[m, :, cols] = acc.astype(BF16)
        return c

    lax.fori_loop(0, width // step, adapters, 0)

    @pl.when(seg == 0)
    def _():
        pltpu.make_async_copy(emb, xbuf, load_sem.at[0]).wait()
        each_micro(lambda m: begin(m, "early"))
        acc[...] = jnp.zeros_like(acc)

    def used(df, ds, hs=(0, 1)):
        @pl.when(seg == 0)
        def _():
            for h in hs:
                start = pl.multiple_of(at(h, df, ds) * block, block)
                for m in range(micro):
                    acc[m, :, h * half : h * half + most] += dot(
                        hbuf[m, :, pl.ds(start, block)], wbuf[h, pl.ds(start, block), :most]
                    )

    def everywhere(step, *which):
        getattr(main, step)(*which)
        on_all_but_opening(lambda: getattr(rest, step)(*which))

    @pl.when(later)
    def _():
        pl.semaphore_wait(turn_sem, 1)
        start_own()

    for h in range(2):
        everywhere("arrived_first", h)

    @pl.when(shared & jnp.logical_not(later))
    def _():
        pl.semaphore_signal(turn_sem, inc=1, device_id=(lax.rem(seg + 1, segments), me), device_id_type=MESH)

    for h in range(2):
        everywhere("spread", h, 1)
        everywhere("spread", h, 2)
    for h in range(2):
        own[h].wait()
    used(0, 0)
    used(-1, 0)
    used(1, 0)
    for h in range(2):
        everywhere("pass_on", h, 0)
    for h in range(2):
        everywhere("first_done", h)
        everywhere("spread", h, 3)
    used(2, 0)
    for i in range(4):
        if i > 0:
            for h in range(2):
                everywhere("pass_on", h, i)
        used(order[i], -1)
        used(order[i], 1)

    @pl.when(opening)
    def _():
        for h in range(2):
            for i in range(4):
                for j in range(4):
                    if i + j > 0:
                        come_back(h, i, j).wait_recv()
            go_over(h).wait_send()

    @pl.when(seg == 0)
    def _():
        for h in range(2):
            for m in range(micro):
                acc[m, :, h * half + most : (h + 1) * half] = dot(hbuf[m], wbuf[h, :, most:])

    for i in range(4):
        for h in range(2):
            everywhere("second_done", h, i)
            used(order[i], 2, (h,))

    @pl.when(seg == 0)
    def _():
        each_micro(lambda m: finish(m, "early"))

    everywhere("sent")

    @pl.when(closing)
    def _():
        visit.sent()
        for h in range(2):
            for i in range(4):
                for j in range(4):
                    if i + j > 0:
                        come_back(h, i, j).wait_send()

    def normed(m):
        def body(q, c):
            h = xbuf[m, :, chunk(q)].astype(F32) * invbuf[m] * gain[:, chunk(q)]
            hbuf[m, :, chunk(q)] = h.astype(BF16)
            return c

        over_chunks(body)

    def adapter_grads(m):
        glow = glowbuf[m]

        def body(q, c):
            seq[m, :, chunk(q)] = dot(glow, hbuf[m, :, chunk(q)], ((0,), (0,)))
            seq[micro + m, :, chunk(q)] = dot(lowbuf[m], gbuf[m, :, chunk(q)], ((0,), (0,)))
            return c

        over_chunks(body)

    def share_all():
        lax.fori_loop(1, members, share_start, 0)

    def backward(m, kind, between=None):
        if kind == "comes":
            acc[m] = jnp.zeros((rows, width), F32)

        def take_in(q, c):
            along, gl = c
            if kind != "rows":
                back(m, q).wait_recv()
            g = gbuf[m, :, chunk(q)]
            if kind == "comes":
                for i in range(2):
                    acc[m, :, i * half : (i + 1) * half] += dot(g, wbuf[i, chunk(q), :])
            change = obuf[m, :, chunk(q)].astype(F32) - xbuf[m, :, chunk(q)].astype(F32)
            along = along + jnp.sum(g.astype(F32) * change, axis=1, keepdims=True)
            return along, gl + dot(g, up[m, :, chunk(q)], ((1,), (1,)))

        along, gl = over_chunks(take_in, (column, narrow))
        glow = gl.astype(BF16)
        glowbuf[m] = glow
        inv = invbuf[m]
        coef = along / width * inv * inv
        if between is not None:

            @pl.when(seg == 0)
            def _():
                between(m)

        at_once = 2 if kind == "rows" else 1

        def give_out(q, c):
            cols = pl.ds(pl.multiple_of(q * at_once * wide, at_once * wide), at_once * wide)
            if kind == "comes":
                dh = acc[m, :, cols]
            elif kind == "columns":
                dh = dot(gbuf[m], by_columns(q))
            else:
                turned = dot(wbuf[0, cols, :], gbuf[m, :, :half], ((1,), (1,)))
                turned = turned + dot(wbuf[1, cols, :], gbuf[m, :, half:], ((1,), (1,)))
                dh = turned.T
            dh = dh + dot(glow, down[m, :, cols])
            out = gbuf[m, :, cols].astype(F32) + inv * (gain[:, cols] * dh)
            gout[m, :, cols] = (out - xbuf[m, :, cols].astype(F32) * coef).astype(BF16)

            @pl.when(seg > 0)
            def _():
                for i in range(at_once):
                    back(m, q * at_once + i).start()

            return c

        lax.fori_loop(0, CHUNKS // at_once, give_out, 0)
        pltpu.make_async_copy(gout.at[m], grads_in.at[m], store_sem.at[micro + m]).start()

    even = lax.rem(seg, 2) == 0

    @pl.when(even & (seg > 0))
    def _():
        each_micro(lambda m: forward(m, "comes"))

    @pl.when(jnp.logical_not(even) & (seg < last))
    def _():
        each_micro(lambda m: forward(m, "columns"))

    @pl.when(seg < last)
    def _():
        each_micro(normed)

        size = 512
        count = width // size

        def place(i, j):
            inner = lax.rem(j, count // 2)
            return wbuf.at[
                j // (count // 2), pl.ds(pl.multiple_of(i * size, size), size), pl.ds(pl.multiple_of(inner * size, size), size)
            ]

        def turn(i, c):
            def inner(j, c):
                a, b = place(i, j)[...].T, place(j, i)[...].T
                place(j, i)[...] = a
                place(i, j)[...] = b
                return c

            return lax.fori_loop(i, count, inner, c)

        lax.fori_loop(0, count, turn, 0)

    def before_the_last(m):
        adapter_grads(m)

        @pl.when(m == micro - 1)
        def _():
            share_all()

    @pl.when(even)
    def _():
        each_micro(lambda m: backward(m, "columns", before_the_last))

    @pl.when(jnp.logical_not(even) & (seg < last))
    def _():
        each_micro(lambda m: backward(m, "comes"))

    @pl.when(seg == last)
    def _():
        pltpu.make_async_copy(cot, gbuf, load_sem.at[1]).wait()

        def both(m):
            keep = lax.broadcasted_iota(jnp.int32, (rows, wide), 0) < lens[m, me]

            def masked(q, c):
                gbuf[m, :, chunk(q)] = jnp.where(keep, gbuf[m, :, chunk(q)].astype(F32), 0.0).astype(BF16)
                return c

            over_chunks(masked)
            forward(m, "columns")
            backward(m, "rows")

        each_micro(both)
        each_micro(normed)

    @pl.when(seg > 0)
    def _():
        each_micro(adapter_grads)
        share_all()

    def add(mine, source, fresh):
        for t, target in enumerate((gdown, gup)):
            for s in range(skills):
                p = sum(mixb[s, pl.ds(m * members + source, 1), :] * mine[t * micro + m] for m in range(micro))
                p = p.astype(BF16).astype(F32)
                target[s] = p if fresh else target[s] + p

    own_cols = pl.ds(pl.multiple_of(me * block, block), block)
    add([seq[i, :, own_cols] for i in range(2 * micro)], me, True)

    def take(d, c):
        share(d).wait_recv()
        add([got[d, i] for i in range(2 * micro)], lax.rem(me - d + members, members), False)
        return c

    lax.fori_loop(1, members, take, 0)

    def drain(d, c):
        share(d).wait_send()
        return c

    lax.fori_loop(1, members, drain, 0)
    for m in range(micro):
        pltpu.make_async_copy(obuf.at[m], hidden.at[m], store_sem.at[m]).wait()
        pltpu.make_async_copy(gout.at[m], grads_in.at[m], store_sem.at[micro + m]).wait()

    @pl.when(seg < last)
    def _():
        for m in range(micro):
            for q in range(CHUNKS):
                onward(m, q).wait_send()

    @pl.when(seg > 0)
    def _():
        for m in range(micro):
            for q in range(CHUNKS):
                back(m, q).wait_send()


def shards(embeds, base_weight, norm_gain, skill_down, skill_up, task_ids, allocation, target_lengths, cotangent):
    micro, _, rows, width = embeds.shape
    block = base_weight.shape[1]
    _, skills, rank, _ = skill_down.shape
    members = lax.axis_size("dp")
    anywhere = pl.BlockSpec(memory_space=pl.ANY)
    vmem = pl.BlockSpec(memory_space=pltpu.VMEM)
    smem = pl.BlockSpec(memory_space=pltpu.SMEM)
    stream = jax.ShapeDtypeStruct((micro, rows, width), BF16)
    grad = jax.ShapeDtypeStruct((skills, rank, block), F32)
    dma = pltpu.SemaphoreType.DMA
    held = pltpu.VMEM((micro, rows, width), BF16)
    hidden, grads_in, gdown, gup = pl.pallas_call(
        kernel,
        out_shape=(stream, stream, grad, grad),
        in_specs=[anywhere, anywhere, vmem, vmem, vmem, vmem, anywhere, smem, anywhere],
        out_specs=(anywhere, anywhere, vmem, vmem),
        scratch_shapes=[
            pltpu.VMEM((2, width, width // 2), BF16),
            pltpu.VMEM((2, width, width // 16), BF16),
            held, held, held, held, held,
            pltpu.VMEM((micro, rank, width), BF16),
            pltpu.VMEM((micro, rank, width), BF16),
            pltpu.VMEM((micro, rows, rank), BF16),
            pltpu.VMEM((micro, rows, rank), BF16),
            pltpu.VMEM((micro, rows, 1), F32),
            pltpu.VMEM((skills, micro * members, block), F32),
            pltpu.VMEM(allocation.shape[::-1], jnp.int32),
            pltpu.VMEM((micro, rows, width), F32),
            pltpu.VMEM((2 * micro, rank, width), F32),
            pltpu.VMEM((members, 2 * micro, rank, block), F32),
            *((dma((2, 4)), dma((2, 4)), dma((2, 4, 4)), dma((2, 4, 4))) * 3),
            dma((2,)), dma((2,)), dma((2, 16)), dma((2, 16)), dma((2,)),
            dma((micro, CHUNKS)), dma((micro, CHUNKS)), dma((micro, CHUNKS)), dma((micro, CHUNKS)),
            dma((3,)), dma((2 * micro,)), dma((members,)), dma((members,)), pltpu.SemaphoreType.REGULAR,
        ],
        compiler_params=pltpu.CompilerParams(
            collective_id=0, has_side_effects=True, vmem_limit_bytes=60 * 1024 * 1024
        ),
    )(
        embeds[:, 0], base_weight[0], norm_gain, skill_down[0], skill_up[0],
        task_ids, allocation.T, target_lengths, cotangent[:, 0],
    )
    return (hidden[None, :, None], grads_in[None, :, None], gdown[None], gup[None])


def solution(mesh):
    in_specs = (
        P(None, "dp", None, None),
        P("segment", "dp", None),
        P("segment", None),
        P("segment", None, None, None),
        P("segment", None, None, None),
        P(),
        P(),
        P(),
        P(None, "dp", None, None),
    )
    out_specs = (
        P("segment", None, "dp", None, None),
        P("segment", None, "dp", None, None),
        P("segment", None, None, "dp"),
        P("segment", None, None, "dp"),
    )
    return jax.shard_map(shards, mesh=mesh, in_specs=in_specs, out_specs=out_specs, check_vma=False)
```

```python
import functools

import jax
import jax.numpy as jnp
from jax import lax
from jax.experimental import pallas as pl
from jax.experimental.pallas import tpu as pltpu
from jax.sharding import PartitionSpec as P

EPS = 1e-06
MESH = pl.DeviceIdType.MESH
SIDE = 4
CHUNKS = 8
F32 = jnp.float32
BF16 = jnp.bfloat16


def dot(a, b, dims=((1,), (0,))):
    return lax.dot_general(a, b, (dims, ((), ())), preferred_element_type=F32)


def kernel(
    emb, w, gain, sdown, sup, tasks, alloc, lens, cot,
    hidden, grads_in, gdown, gup,
    wbuf, vis, xbuf, obuf, hbuf, gbuf, gout, down, up, lowbuf, glowbuf, invbuf, mixb, table, acc, seq, got,
    *sems,
):
    main_sems, rest_sems, visit_sems = sems[:4], sems[4:8], sems[8:12]
    over_s, over_r, back_s, back_r, own_sem = sems[12:17]
    x_s, x_r, g_s, g_r, load_sem, store_sem, seq_s, seq_r, turn_sem = sems[17:]
    segments = lax.axis_size("segment")
    members = lax.axis_size("dp")
    seg = lax.axis_index("segment")
    me = lax.axis_index("dp")
    micro, rows, width = emb.shape
    block = w.shape[0]
    half = width // 2
    part = block // 2
    skills, rank = sdown.shape[0], sdown.shape[1]
    z, y = me // SIDE, lax.rem(me, SIDE)
    last = segments - 1

    barrier = pltpu.get_barrier_semaphore()

    def greet(d, c):
        pl.semaphore_signal(barrier, inc=1, device_id=(seg, lax.rem(me + d, members)), device_id_type=MESH)
        return c

    lax.fori_loop(1, members, greet, 0)
    for d in (1, 2, segments - 2, segments - 1):
        pl.semaphore_signal(barrier, inc=1, device_id=(lax.rem(seg + d, segments), me), device_id_type=MESH)
    pl.semaphore_wait(barrier, members + 3)

    wide = width // CHUNKS

    def chunk(q):
        return pl.ds(pl.multiple_of(q * wide, wide), wide)

    def columns_of(q, at_once):
        size = at_once * wide
        return pl.ds(pl.multiple_of(q * size, size), size)

    def by_columns(q, at_once=1):
        count = half // (at_once * wide)
        return wbuf[q // count, :, columns_of(lax.rem(q, count), at_once)]

    def hop(buf, target, m, q, s, r, to):
        return pltpu.make_async_remote_copy(
            src_ref=buf.at[m, :, chunk(q)], dst_ref=target.at[m, :, chunk(q)], send_sem=s.at[m, q], recv_sem=r.at[m, q],
            device_id=(to, me), device_id_type=MESH,
        )

    onward = functools.partial(hop, obuf, xbuf, s=x_s, r=x_r, to=lax.rem(seg + 1, segments))
    back = functools.partial(hop, gout, gbuf, s=g_s, r=g_r, to=lax.rem(seg + last, segments))
    column = jnp.zeros((rows, 1), F32)
    narrow = jnp.zeros((rows, rank), F32)

    def share(d):
        to = lax.rem(me + d, members)
        return pltpu.make_async_remote_copy(
            src_ref=seq.at[:, :, pl.ds(pl.multiple_of(to * block, block), block)], dst_ref=got.at[d],
            send_sem=seq_s.at[d], recv_sem=seq_r.at[d], device_id=(seg, to), device_id_type=MESH,
        )

    def share_start(d, c):
        share(d).start()
        return c

    def over_chunks(body, init=0):
        return lax.fori_loop(0, CHUNKS, body, init)

    def each_micro(body):
        def step(m, c):
            body(m)
            return c

        lax.fori_loop(0, micro, step, 0)

    def begin(m, kind):
        if kind == "comes":
            acc[m] = jnp.zeros((rows, width), F32)

        def take_in(q, c):
            ss, lw = c
            if kind != "early":

                @pl.when(seg > 0)
                def _():
                    onward(m, q).wait_recv()

            v = xbuf[m, :, chunk(q)].astype(F32)
            h = (v * gain[:, chunk(q)]).astype(BF16)
            if kind == "comes":
                for i in range(2):
                    acc[m, :, i * half : (i + 1) * half] += dot(h, wbuf[i, chunk(q), :])
            else:
                hbuf[m, :, chunk(q)] = h
            return ss + jnp.sum(v * v, axis=1, keepdims=True), lw + dot(h, down[m, :, chunk(q)], ((1,), (1,)))

        ss, lw = over_chunks(take_in, (column, narrow))
        inv = lax.rsqrt(ss / width + EPS)
        invbuf[m] = inv
        lowbuf[m] = (lw * inv).astype(BF16)

    def finish(m, kind):
        inv = invbuf[m]
        low = lowbuf[m]

        at_once = 2 if kind == "wide" else 1

        def give_out(q, c):
            cols = columns_of(q, at_once)
            total = dot(hbuf[m], by_columns(q, at_once)) if kind in ("columns", "wide") else acc[m, :, cols]
            total = xbuf[m, :, cols].astype(F32) + inv * total + dot(low, up[m, :, cols])
            obuf[m, :, cols] = total.astype(BF16)
            if kind != "wide":

                @pl.when(seg < last)
                def _():
                    onward(m, q).start()

            return c

        lax.fori_loop(0, CHUNKS // at_once, give_out, 0)
        pltpu.make_async_copy(obuf.at[m], hidden.at[m], store_sem.at[m]).start()

    def forward(m, kind):
        begin(m, kind)
        finish(m, kind)

    extra = vis.shape[2]
    most = half - extra
    order = (0, -1, 1, 2)
    ways = (1, -1)
    opening = seg < 2
    closing = seg >= segments - 2

    def at(h, df, ds):
        dy, dz = (df, ds) if h == 0 else (ds, df)
        return lax.rem(z + dz + SIDE, SIDE) * SIDE + lax.rem(y + dy + SIDE, SIDE)

    def block_of(buf, cols, h, df, ds, sub=None):
        start = at(h, df, ds) * block
        if sub is None:
            return buf.at[h, pl.ds(pl.multiple_of(start, block), block), cols]
        return buf.at[h, pl.ds(pl.multiple_of(start + sub * part, part), part), cols]

    def remote(src, dst, s, r, to, to_seg=seg):
        return pltpu.make_async_remote_copy(
            src_ref=src, dst_ref=dst, send_sem=s, recv_sem=r, device_id=(to_seg, to), device_id_type=MESH
        )

    class Stream:
        def __init__(self, buf, cols, mine, f_s, f_r, s_s, s_r):
            self.ref = functools.partial(block_of, buf, cols)
            self.mine, self.sems = mine, (f_s, f_r, s_s, s_r)

        def first(self, h, d):
            way = ways[d % 2]
            dst = self.ref(h, 0, 0) if d < 2 else self.ref(h, -way, 0, d - 2)
            src = self.mine(h) if d < 2 else dst
            return remote(src, dst, self.sems[0].at[h, d], self.sems[1].at[h, d], at(h, way, 0))

        def second(self, h, i, d):
            way = ways[d % 2]
            dst = self.ref(h, order[i], 0) if d < 2 else self.ref(h, order[i], -way, d - 2)
            src = self.mine(h) if d < 2 and i == 0 else dst
            return remote(src, dst, self.sems[2].at[h, i, d], self.sems[3].at[h, i, d], at(h, 0, way))

        def open(self):
            for h in range(2):
                for d in range(2):
                    self.first(h, d).start()
            for h in range(2):
                self.spread(h, 0)

        def arrived_first(self, h):
            for d in range(2):
                self.first(h, d).wait_recv()
                self.first(h, 2 + d).start()

        def spread(self, h, i):
            for d in range(2):
                self.second(h, i, d).start()

        def pass_on(self, h, i):
            for d in range(2):
                self.second(h, i, d).wait_recv()
                self.second(h, i, 2 + d).start()

        def first_done(self, h):
            for d in range(2):
                self.first(h, 2 + d).wait_recv()

        def second_done(self, h, i):
            for d in range(2):
                self.second(h, i, 2 + d).wait_recv()

        def sent(self):
            for h in range(2):
                for d in range(4):
                    self.first(h, d).wait_send()
                    for i in range(4):
                        self.second(h, i, d).wait_send()

    side = pl.ds(most, extra)
    main = Stream(wbuf, pl.ds(0, most), lambda h: w.at[:, pl.ds(h * half, most)], *main_sems)
    rest = Stream(wbuf, side, lambda h: w.at[:, pl.ds(h * half + most, extra)], *rest_sems)
    visit = Stream(vis, pl.ds(0, extra), lambda h: block_of(vis, pl.ds(0, extra), h, 0, 0), *visit_sems)

    def go_over(h):
        return remote(
            w.at[:, pl.ds(h * half + most, extra)], block_of(vis, pl.ds(0, extra), h, 0, 0),
            over_s.at[h], over_r.at[h], me, lax.rem(seg + segments - 2, segments),
        )

    def come_back(h, i, j):
        return remote(
            block_of(vis, pl.ds(0, extra), h, order[i], order[j]), block_of(wbuf, side, h, order[i], order[j]),
            back_s.at[h, i * 4 + j], back_r.at[h, i * 4 + j], me, lax.rem(seg + 2, segments),
        )

    def on_all_but_opening(body):
        pl.when(jnp.logical_not(opening))(body)

    def start_own():
        main.open()
        on_all_but_opening(rest.open)

    @pl.when(opening)
    def _():
        for h in range(2):
            go_over(h).start()

    shared = seg >= 2
    later = shared & (lax.rem(seg, 2) == 1)

    @pl.when(jnp.logical_not(closing) & jnp.logical_not(later))
    def _():
        start_own()

    own = []
    for h in range(2):
        c = pltpu.make_async_copy(
            w.at[:, h * half : (h + 1) * half], block_of(wbuf, pl.ds(0, half), h, 0, 0), own_sem.at[h]
        )
        c.start()
        own.append(c)
    pltpu.make_async_copy(alloc, table, load_sem.at[2]).start()

    @pl.when(seg == 0)
    def _():
        pltpu.make_async_copy(emb, xbuf, load_sem.at[0]).start()

    @pl.when(seg == last)
    def _():
        pltpu.make_async_copy(cot, gbuf, load_sem.at[1]).start()


    @pl.when(closing)
    def _():
        for h in range(2):
            go_over(h).wait_recv()
        visit.open()
        pl.when(jnp.logical_not(later))(start_own)
        for h in range(2):
            visit.arrived_first(h)
        for h in range(2):
            visit.spread(h, 1)
            visit.spread(h, 2)
        for h in range(2):
            come_back(h, 1, 0).start()
            come_back(h, 2, 0).start()
            visit.pass_on(h, 0)
        for h in range(2):
            visit.first_done(h)
            visit.spread(h, 3)
        for i in range(4):
            for h in range(2):
                if i > 0:
                    visit.pass_on(h, i)
                come_back(h, i, 1).start()
                come_back(h, i, 2).start()
        for h in range(2):
            come_back(h, 3, 0).start()
        for i in range(4):
            for h in range(2):
                visit.second_done(h, i)
                come_back(h, i, 3).start()

    pltpu.make_async_copy(alloc, table, load_sem.at[2]).wait()
    known = table[...].astype(F32).astype(BF16)
    for m in range(micro):
        picked = lax.broadcasted_iota(jnp.int32, (table.shape[1], members), 0) == tasks[m : m + 1, :]
        uses = dot(picked.astype(F32).astype(BF16), known, ((0,), (1,)))
        mix = uses / jnp.maximum(jnp.sum(uses, axis=1, keepdims=True), 1.0)
        for s in range(skills):
            mixb[s, m * members : (m + 1) * members] = jnp.broadcast_to(mix[:, s : s + 1], (members, mixb.shape[2]))
    step = mixb.shape[2]

    def adapters(i, c):
        cols = pl.ds(pl.multiple_of(i * step, step), step)
        for m in range(micro):
            for source, target in ((sdown, down), (sup, up)):
                acc = jnp.zeros((rank, step), F32)
                for s in range(skills):
                    acc = acc + mixb[s, pl.ds(m * members + me, 1), :] * source[s, :, cols].astype(F32)
                target[m, :, cols] = acc.astype(BF16)
        return c

    lax.fori_loop(0, width // step, adapters, 0)

    @pl.when(seg == 0)
    def _():
        pltpu.make_async_copy(emb, xbuf, load_sem.at[0]).wait()
        each_micro(lambda m: begin(m, "early"))
        acc[...] = jnp.zeros_like(acc)

    def used(df, ds, hs=(0, 1)):
        @pl.when(seg == 0)
        def _():
            for h in hs:
                start = pl.multiple_of(at(h, df, ds) * block, block)
                for m in range(micro):
                    acc[m, :, h * half : h * half + most] += dot(
                        hbuf[m, :, pl.ds(start, block)], wbuf[h, pl.ds(start, block), :most]
                    )

    def everywhere(step, *which):
        getattr(main, step)(*which)
        on_all_but_opening(lambda: getattr(rest, step)(*which))

    @pl.when(later)
    def _():
        pl.semaphore_wait(turn_sem, 1)
        start_own()

    for h in range(2):
        everywhere("arrived_first", h)

    @pl.when(shared & jnp.logical_not(later))
    def _():
        pl.semaphore_signal(turn_sem, inc=1, device_id=(lax.rem(seg + 1, segments), me), device_id_type=MESH)

    for h in range(2):
        everywhere("spread", h, 1)
        everywhere("spread", h, 2)
    for h in range(2):
        own[h].wait()
    used(0, 0)
    used(-1, 0)
    used(1, 0)
    for h in range(2):
        everywhere("pass_on", h, 0)
    for h in range(2):
        everywhere("first_done", h)
        everywhere("spread", h, 3)
    used(2, 0)
    for i in range(4):
        if i > 0:
            for h in range(2):
                everywhere("pass_on", h, i)
        used(order[i], -1)
        used(order[i], 1)

    @pl.when(opening)
    def _():
        for h in range(2):
            for i in range(4):
                for j in range(4):
                    if i + j > 0:
                        come_back(h, i, j).wait_recv()
            go_over(h).wait_send()

    @pl.when(seg == 0)
    def _():
        for h in range(2):
            for m in range(micro):
                acc[m, :, h * half + most : (h + 1) * half] = dot(hbuf[m], wbuf[h, :, most:])

    for i in range(4):
        for h in range(2):
            everywhere("second_done", h, i)
            used(order[i], 2, (h,))

    @pl.when(seg == 0)
    def _():
        each_micro(lambda m: finish(m, "early"))

    everywhere("sent")

    @pl.when(closing)
    def _():
        visit.sent()
        for h in range(2):
            for i in range(4):
                for j in range(4):
                    if i + j > 0:
                        come_back(h, i, j).wait_send()

    def normed(m):
        def body(q, c):
            h = xbuf[m, :, chunk(q)].astype(F32) * invbuf[m] * gain[:, chunk(q)]
            hbuf[m, :, chunk(q)] = h.astype(BF16)
            return c

        over_chunks(body)

    def adapter_grads(m):
        glow = glowbuf[m]

        def body(q, c):
            seq[m, :, chunk(q)] = dot(glow, hbuf[m, :, chunk(q)], ((0,), (0,)))
            seq[micro + m, :, chunk(q)] = dot(lowbuf[m], gbuf[m, :, chunk(q)], ((0,), (0,)))
            return c

        over_chunks(body)

    def share_all():
        lax.fori_loop(1, members, share_start, 0)

    def backward(m, kind, between=None):
        if kind == "comes":
            acc[m] = jnp.zeros((rows, width), F32)

        def take_in(q, c):
            along, gl = c
            if kind != "rows":
                back(m, q).wait_recv()
            g = gbuf[m, :, chunk(q)]
            if kind == "comes":
                for i in range(2):
                    acc[m, :, i * half : (i + 1) * half] += dot(g, wbuf[i, chunk(q), :])
            change = obuf[m, :, chunk(q)].astype(F32) - xbuf[m, :, chunk(q)].astype(F32)
            along = along + jnp.sum(g.astype(F32) * change, axis=1, keepdims=True)
            if kind == "rows":
                return along, gl
            return along, gl + dot(g, up[m, :, chunk(q)], ((1,), (1,)))

        along, gl = over_chunks(take_in, (column, narrow))
        if kind != "rows":
            glowbuf[m] = gl.astype(BF16)
        glow = glowbuf[m]
        inv = invbuf[m]
        coef = along / width * inv * inv
        if between is not None:
            between(m)
        at_once = 2 if kind in ("rows", "wide") else 1

        def give_out(q, c):
            cols = columns_of(q, at_once)
            if kind == "comes":
                dh = acc[m, :, cols]
            elif kind in ("columns", "wide"):
                dh = dot(gbuf[m], by_columns(q, at_once))
            else:
                turned = dot(wbuf[0, cols, :], gbuf[m, :, :half], ((1,), (1,)))
                turned = turned + dot(wbuf[1, cols, :], gbuf[m, :, half:], ((1,), (1,)))
                dh = turned.T
            dh = dh + dot(glow, down[m, :, cols])
            out = gbuf[m, :, cols].astype(F32) + inv * (gain[:, cols] * dh)
            gout[m, :, cols] = (out - xbuf[m, :, cols].astype(F32) * coef).astype(BF16)

            @pl.when(seg > 0)
            def _():
                for i in range(at_once):
                    back(m, q * at_once + i).start()

            return c

        lax.fori_loop(0, CHUNKS // at_once, give_out, 0)
        pltpu.make_async_copy(gout.at[m], grads_in.at[m], store_sem.at[micro + m]).start()

    even = lax.rem(seg, 2) == 0

    @pl.when(even & (seg > 0))
    def _():
        each_micro(lambda m: forward(m, "comes"))

    @pl.when(jnp.logical_not(even) & (seg < last))
    def _():
        each_micro(lambda m: forward(m, "columns"))

    @pl.when(seg < last)
    def _():
        each_micro(normed)

        size = 512
        count = width // size

        def place(i, j):
            inner = lax.rem(j, count // 2)
            return wbuf.at[
                j // (count // 2), pl.ds(pl.multiple_of(i * size, size), size), pl.ds(pl.multiple_of(inner * size, size), size)
            ]

        def turn(i, c):
            def inner(j, c):
                a, b = place(i, j)[...].T, place(j, i)[...].T
                place(j, i)[...] = a
                place(i, j)[...] = b
                return c

            return lax.fori_loop(i, count, inner, c)

        lax.fori_loop(0, count, turn, 0)

    def before_the_last(m):
        adapter_grads(m)

        @pl.when(m == micro - 1)
        def _():
            share_all()

    def and_grads(m, kind):
        backward(m, kind)
        adapter_grads(m)

    @pl.when(seg == 0)
    def _():
        each_micro(lambda m: backward(m, "wide", before_the_last))

    @pl.when(even & (seg > 0))
    def _():
        each_micro(lambda m: and_grads(m, "columns"))

    @pl.when(jnp.logical_not(even) & (seg < last))
    def _():
        each_micro(lambda m: and_grads(m, "comes"))

    @pl.when(seg == last)
    def _():
        pltpu.make_async_copy(cot, gbuf, load_sem.at[1]).wait()

        def ready(m):
            keep = lax.broadcasted_iota(jnp.int32, (rows, wide), 0) < lens[m, me]

            def masked(q, c):
                gbuf[m, :, chunk(q)] = jnp.where(keep, gbuf[m, :, chunk(q)].astype(F32), 0.0).astype(BF16)
                return c

            over_chunks(masked)
            glowbuf[m] = dot(gbuf[m], up[m], ((1,), (1,))).astype(BF16)

        def both(m):
            forward(m, "wide")
            backward(m, "rows")

        each_micro(ready)
        each_micro(both)
        each_micro(normed)
        each_micro(adapter_grads)

    @pl.when(seg > 0)
    def _():
        share_all()

    def add(mine, source, fresh):
        for t, target in enumerate((gdown, gup)):
            for s in range(skills):
                p = sum(mixb[s, pl.ds(m * members + source, 1), :] * mine[t * micro + m] for m in range(micro))
                p = p.astype(BF16).astype(F32)
                target[s] = p if fresh else target[s] + p

    own_cols = pl.ds(pl.multiple_of(me * block, block), block)
    add([seq[i, :, own_cols] for i in range(2 * micro)], me, True)

    def take(d, c):
        share(d).wait_recv()
        add([got[d, i] for i in range(2 * micro)], lax.rem(me - d + members, members), False)
        return c

    lax.fori_loop(1, members, take, 0)

    def drain(d, c):
        share(d).wait_send()
        return c

    lax.fori_loop(1, members, drain, 0)
    for m in range(micro):
        pltpu.make_async_copy(obuf.at[m], hidden.at[m], store_sem.at[m]).wait()
        pltpu.make_async_copy(gout.at[m], grads_in.at[m], store_sem.at[micro + m]).wait()

    @pl.when(seg < last)
    def _():
        for m in range(micro):
            for q in range(CHUNKS):
                onward(m, q).wait_send()

    @pl.when(seg > 0)
    def _():
        for m in range(micro):
            for q in range(CHUNKS):
                back(m, q).wait_send()


def shards(embeds, base_weight, norm_gain, skill_down, skill_up, task_ids, allocation, target_lengths, cotangent):
    micro, _, rows, width = embeds.shape
    block = base_weight.shape[1]
    _, skills, rank, _ = skill_down.shape
    members = lax.axis_size("dp")
    anywhere = pl.BlockSpec(memory_space=pl.ANY)
    vmem = pl.BlockSpec(memory_space=pltpu.VMEM)
    smem = pl.BlockSpec(memory_space=pltpu.SMEM)
    stream = jax.ShapeDtypeStruct((micro, rows, width), BF16)
    grad = jax.ShapeDtypeStruct((skills, rank, block), F32)
    dma = pltpu.SemaphoreType.DMA
    held = pltpu.VMEM((micro, rows, width), BF16)
    hidden, grads_in, gdown, gup = pl.pallas_call(
        kernel,
        out_shape=(stream, stream, grad, grad),
        in_specs=[anywhere, anywhere, vmem, vmem, vmem, vmem, anywhere, smem, anywhere],
        out_specs=(anywhere, anywhere, vmem, vmem),
        scratch_shapes=[
            pltpu.VMEM((2, width, width // 2), BF16),
            pltpu.VMEM((2, width, width // 16), BF16),
            held, held, held, held, held,
            pltpu.VMEM((micro, rank, width), BF16),
            pltpu.VMEM((micro, rank, width), BF16),
            pltpu.VMEM((micro, rows, rank), BF16),
            pltpu.VMEM((micro, rows, rank), BF16),
            pltpu.VMEM((micro, rows, 1), F32),
            pltpu.VMEM((skills, micro * members, block), F32),
            pltpu.VMEM(allocation.shape[::-1], jnp.int32),
            pltpu.VMEM((micro, rows, width), F32),
            pltpu.VMEM((2 * micro, rank, width), F32),
            pltpu.VMEM((members, 2 * micro, rank, block), F32),
            *((dma((2, 4)), dma((2, 4)), dma((2, 4, 4)), dma((2, 4, 4))) * 3),
            dma((2,)), dma((2,)), dma((2, 16)), dma((2, 16)), dma((2,)),
            dma((micro, CHUNKS)), dma((micro, CHUNKS)), dma((micro, CHUNKS)), dma((micro, CHUNKS)),
            dma((3,)), dma((2 * micro,)), dma((members,)), dma((members,)), pltpu.SemaphoreType.REGULAR,
        ],
        compiler_params=pltpu.CompilerParams(
            collective_id=0, has_side_effects=True, vmem_limit_bytes=60 * 1024 * 1024
        ),
    )(
        embeds[:, 0], base_weight[0], norm_gain, skill_down[0], skill_up[0],
        task_ids, allocation.T, target_lengths, cotangent[:, 0],
    )
    return (hidden[None, :, None], grads_in[None, :, None], gdown[None], gup[None])


def solution(mesh):
    in_specs = (
        P(None, "dp", None, None),
        P("segment", "dp", None),
        P("segment", None),
        P("segment", None, None, None),
        P("segment", None, None, None),
        P(),
        P(),
        P(),
        P(None, "dp", None, None),
    )
    out_specs = (
        P("segment", None, "dp", None, None),
        P("segment", None, "dp", None, None),
        P("segment", None, None, "dp"),
        P("segment", None, None, "dp"),
    )
    return jax.shard_map(shards, mesh=mesh, in_specs=in_specs, out_specs=out_specs, check_vma=False)
```

```python
import functools

import jax
import jax.numpy as jnp
from jax import lax
from jax.experimental import pallas as pl
from jax.experimental.pallas import tpu as pltpu
from jax.sharding import PartitionSpec as P

EPS = 1e-06
MESH = pl.DeviceIdType.MESH
SIDE = 4
CHUNKS = 8
F32 = jnp.float32
BF16 = jnp.bfloat16


def dot(a, b, dims=((1,), (0,))):
    return lax.dot_general(a, b, (dims, ((), ())), preferred_element_type=F32)


def kernel(
    emb, w, gain, sdown, sup, tasks, alloc, lens, cot,
    hidden, grads_in, gdown, gup,
    wbuf, vis, xbuf, obuf, hbuf, gbuf, gout, down, up, lowbuf, glowbuf, invbuf, mixb, table, acc, seq, got,
    *sems,
):
    main_sems, rest_sems, visit_sems = sems[:4], sems[4:8], sems[8:12]
    over_s, over_r, back_s, back_r, own_sem = sems[12:17]
    x_s, x_r, g_s, g_r, load_sem, store_sem, seq_s, seq_r, turn_sem = sems[17:]
    segments = lax.axis_size("segment")
    members = lax.axis_size("dp")
    seg = lax.axis_index("segment")
    me = lax.axis_index("dp")
    micro, rows, width = emb.shape
    block = w.shape[0]
    half = width // 2
    part = block // 2
    skills, rank = sdown.shape[0], sdown.shape[1]
    z, y = me // SIDE, lax.rem(me, SIDE)
    last = segments - 1

    barrier = pltpu.get_barrier_semaphore()

    def greet(d, c):
        pl.semaphore_signal(barrier, inc=1, device_id=(seg, lax.rem(me + d, members)), device_id_type=MESH)
        return c

    lax.fori_loop(1, members, greet, 0)
    for d in (1, 2, segments - 2, segments - 1):
        pl.semaphore_signal(barrier, inc=1, device_id=(lax.rem(seg + d, segments), me), device_id_type=MESH)
    pl.semaphore_wait(barrier, members + 3)

    wide = width // CHUNKS

    def chunk(q):
        return pl.ds(pl.multiple_of(q * wide, wide), wide)

    def columns_of(q, at_once):
        size = at_once * wide
        return pl.ds(pl.multiple_of(q * size, size), size)

    def by_columns(q, at_once=1):
        count = half // (at_once * wide)
        return wbuf[q // count, :, columns_of(lax.rem(q, count), at_once)]

    def hop(buf, target, m, q, size, s, r, to):
        cols = columns_of(q, size)
        return pltpu.make_async_remote_copy(
            src_ref=buf.at[m, :, cols], dst_ref=target.at[m, :, cols], send_sem=s.at[m, q], recv_sem=r.at[m, q],
            device_id=(to, me), device_id_type=MESH,
        )

    onward = functools.partial(hop, obuf, xbuf, s=x_s, r=x_r, to=lax.rem(seg + 1, segments))
    back = functools.partial(hop, gout, gbuf, s=g_s, r=g_r, to=lax.rem(seg + last, segments))
    column = jnp.zeros((rows, 1), F32)
    narrow = jnp.zeros((rows, rank), F32)

    def share(d):
        to = lax.rem(me + d, members)
        return pltpu.make_async_remote_copy(
            src_ref=seq.at[:, :, pl.ds(pl.multiple_of(to * block, block), block)], dst_ref=got.at[d],
            send_sem=seq_s.at[d], recv_sem=seq_r.at[d], device_id=(seg, to), device_id_type=MESH,
        )

    def share_start(d, c):
        share(d).start()
        return c

    def over_chunks(body, init=0):
        return lax.fori_loop(0, CHUNKS, body, init)

    def each_micro(body):
        def step(m, c):
            body(m)
            return c

        lax.fori_loop(0, micro, step, 0)

    def begin(m, kind):
        if kind == "comes":
            acc[m] = jnp.zeros((rows, width), F32)

        size = 2 if kind in ("columns", "wide") else 1

        def take_in(q, c):
            ss, lw = c
            if kind != "early":
                onward(m, q, size).wait_recv()
            cols = columns_of(q, size)
            v = xbuf[m, :, cols].astype(F32)
            h = (v * gain[:, cols]).astype(BF16)
            if kind == "comes":
                for i in range(2):
                    acc[m, :, i * half : (i + 1) * half] += dot(h, wbuf[i, cols, :])
            else:
                hbuf[m, :, cols] = h
            return ss + jnp.sum(v * v, axis=1, keepdims=True), lw + dot(h, down[m, :, cols], ((1,), (1,)))

        ss, lw = lax.fori_loop(0, CHUNKS // size, take_in, (column, narrow))
        inv = lax.rsqrt(ss / width + EPS)
        invbuf[m] = inv
        lowbuf[m] = (lw * inv).astype(BF16)

    def finish(m, kind):
        inv = invbuf[m]
        low = lowbuf[m]

        at_once = 1 if kind == "columns" else 2

        def give_out(q, c):
            cols = columns_of(q, at_once)
            total = dot(hbuf[m], by_columns(q, at_once)) if kind in ("columns", "wide") else acc[m, :, cols]
            total = xbuf[m, :, cols].astype(F32) + inv * total + dot(low, up[m, :, cols])
            obuf[m, :, cols] = total.astype(BF16)
            if kind != "wide":
                onward(m, q, at_once).start()
            return c

        lax.fori_loop(0, CHUNKS // at_once, give_out, 0)
        pltpu.make_async_copy(obuf.at[m], hidden.at[m], store_sem.at[m]).start()

    def forward(m, kind):
        begin(m, kind)
        finish(m, kind)

    extra = vis.shape[2]
    most = half - extra
    order = (0, -1, 1, 2)
    ways = (1, -1)
    opening = seg < 2
    closing = seg >= segments - 2

    def at(h, df, ds):
        dy, dz = (df, ds) if h == 0 else (ds, df)
        return lax.rem(z + dz + SIDE, SIDE) * SIDE + lax.rem(y + dy + SIDE, SIDE)

    def block_of(buf, cols, h, df, ds, sub=None):
        start = at(h, df, ds) * block
        if sub is None:
            return buf.at[h, pl.ds(pl.multiple_of(start, block), block), cols]
        return buf.at[h, pl.ds(pl.multiple_of(start + sub * part, part), part), cols]

    def remote(src, dst, s, r, to, to_seg=seg):
        return pltpu.make_async_remote_copy(
            src_ref=src, dst_ref=dst, send_sem=s, recv_sem=r, device_id=(to_seg, to), device_id_type=MESH
        )

    class Stream:
        def __init__(self, buf, cols, mine, f_s, f_r, s_s, s_r):
            self.ref = functools.partial(block_of, buf, cols)
            self.mine, self.sems = mine, (f_s, f_r, s_s, s_r)

        def first(self, h, d):
            way = ways[d % 2]
            dst = self.ref(h, 0, 0) if d < 2 else self.ref(h, -way, 0, d - 2)
            src = self.mine(h) if d < 2 else dst
            return remote(src, dst, self.sems[0].at[h, d], self.sems[1].at[h, d], at(h, way, 0))

        def second(self, h, i, d):
            way = ways[d % 2]
            dst = self.ref(h, order[i], 0) if d < 2 else self.ref(h, order[i], -way, d - 2)
            src = self.mine(h) if d < 2 and i == 0 else dst
            return remote(src, dst, self.sems[2].at[h, i, d], self.sems[3].at[h, i, d], at(h, 0, way))

        def open(self):
            for h in range(2):
                for d in range(2):
                    self.first(h, d).start()
            for h in range(2):
                self.spread(h, 0)

        def arrived_first(self, h):
            for d in range(2):
                self.first(h, d).wait_recv()
                self.first(h, 2 + d).start()

        def spread(self, h, i):
            for d in range(2):
                self.second(h, i, d).start()

        def pass_on(self, h, i):
            for d in range(2):
                self.second(h, i, d).wait_recv()
                self.second(h, i, 2 + d).start()

        def first_done(self, h):
            for d in range(2):
                self.first(h, 2 + d).wait_recv()

        def second_done(self, h, i):
            for d in range(2):
                self.second(h, i, 2 + d).wait_recv()

        def sent(self):
            for h in range(2):
                for d in range(4):
                    self.first(h, d).wait_send()
                    for i in range(4):
                        self.second(h, i, d).wait_send()

    side = pl.ds(most, extra)
    main = Stream(wbuf, pl.ds(0, most), lambda h: w.at[:, pl.ds(h * half, most)], *main_sems)
    rest = Stream(wbuf, side, lambda h: w.at[:, pl.ds(h * half + most, extra)], *rest_sems)
    visit = Stream(vis, pl.ds(0, extra), lambda h: block_of(vis, pl.ds(0, extra), h, 0, 0), *visit_sems)

    def go_over(h):
        return remote(
            w.at[:, pl.ds(h * half + most, extra)], block_of(vis, pl.ds(0, extra), h, 0, 0),
            over_s.at[h], over_r.at[h], me, lax.rem(seg + segments - 2, segments),
        )

    def come_back(h, i, j):
        return remote(
            block_of(vis, pl.ds(0, extra), h, order[i], order[j]), block_of(wbuf, side, h, order[i], order[j]),
            back_s.at[h, i * 4 + j], back_r.at[h, i * 4 + j], me, lax.rem(seg + 2, segments),
        )

    def on_all_but_opening(body):
        pl.when(jnp.logical_not(opening))(body)

    def start_own():
        main.open()
        on_all_but_opening(rest.open)

    @pl.when(opening)
    def _():
        for h in range(2):
            go_over(h).start()

    shared = seg >= 2
    later = shared & (lax.rem(seg, 2) == 1)

    @pl.when(jnp.logical_not(closing) & jnp.logical_not(later))
    def _():
        start_own()

    own = []
    for h in range(2):
        c = pltpu.make_async_copy(
            w.at[:, h * half : (h + 1) * half], block_of(wbuf, pl.ds(0, half), h, 0, 0), own_sem.at[h]
        )
        c.start()
        own.append(c)
    pltpu.make_async_copy(alloc, table, load_sem.at[2]).start()

    @pl.when(seg == 0)
    def _():
        pltpu.make_async_copy(emb, xbuf, load_sem.at[0]).start()

    @pl.when(seg == last)
    def _():
        pltpu.make_async_copy(cot, gbuf, load_sem.at[1]).start()


    @pl.when(closing)
    def _():
        for h in range(2):
            go_over(h).wait_recv()
        visit.open()
        pl.when(jnp.logical_not(later))(start_own)
        for h in range(2):
            visit.arrived_first(h)
        for h in range(2):
            visit.spread(h, 1)
            visit.spread(h, 2)
        for h in range(2):
            come_back(h, 1, 0).start()
            come_back(h, 2, 0).start()
            visit.pass_on(h, 0)
        for h in range(2):
            visit.first_done(h)
            visit.spread(h, 3)
        for i in range(4):
            for h in range(2):
                if i > 0:
                    visit.pass_on(h, i)
                come_back(h, i, 1).start()
                come_back(h, i, 2).start()
        for h in range(2):
            come_back(h, 3, 0).start()
        for i in range(4):
            for h in range(2):
                visit.second_done(h, i)
                come_back(h, i, 3).start()

    def everywhere(step, *which):
        getattr(main, step)(*which)
        on_all_but_opening(lambda: getattr(rest, step)(*which))

    @pl.when(jnp.logical_not(later))
    def _():
        for h in range(2):
            everywhere("arrived_first", h)

    @pl.when(shared & jnp.logical_not(later))
    def _():
        pl.semaphore_signal(turn_sem, inc=1, device_id=(lax.rem(seg + 1, segments), me), device_id_type=MESH)

    pltpu.make_async_copy(alloc, table, load_sem.at[2]).wait()
    known = table[...].astype(F32).astype(BF16)
    for m in range(micro):
        picked = lax.broadcasted_iota(jnp.int32, (table.shape[1], members), 0) == tasks[m : m + 1, :]
        uses = dot(picked.astype(F32).astype(BF16), known, ((0,), (1,)))
        mix = uses / jnp.maximum(jnp.sum(uses, axis=1, keepdims=True), 1.0)
        for s in range(skills):
            mixb[s, m * members : (m + 1) * members] = jnp.broadcast_to(mix[:, s : s + 1], (members, mixb.shape[2]))
    step = mixb.shape[2]

    def adapters(i, c):
        cols = pl.ds(pl.multiple_of(i * step, step), step)
        for m in range(micro):
            for source, target in ((sdown, down), (sup, up)):
                acc = jnp.zeros((rank, step), F32)
                for s in range(skills):
                    acc = acc + mixb[s, pl.ds(m * members + me, 1), :] * source[s, :, cols].astype(F32)
                target[m, :, cols] = acc.astype(BF16)
        return c

    lax.fori_loop(0, width // step, adapters, 0)

    @pl.when(later)
    def _():
        pl.semaphore_wait(turn_sem, 1)
        start_own()
        for h in range(2):
            everywhere("arrived_first", h)

    @pl.when(seg == 0)
    def _():
        pltpu.make_async_copy(emb, xbuf, load_sem.at[0]).wait()
        each_micro(lambda m: begin(m, "early"))
        acc[...] = jnp.zeros_like(acc)

    def used(df, ds, hs=(0, 1)):
        @pl.when(seg == 0)
        def _():
            for h in hs:
                start = pl.multiple_of(at(h, df, ds) * block, block)
                for m in range(micro):
                    acc[m, :, h * half : h * half + most] += dot(
                        hbuf[m, :, pl.ds(start, block)], wbuf[h, pl.ds(start, block), :most]
                    )

    for h in range(2):
        everywhere("spread", h, 1)
        everywhere("spread", h, 2)
    for h in range(2):
        own[h].wait()
    used(0, 0)
    used(-1, 0)
    used(1, 0)
    for h in range(2):
        everywhere("pass_on", h, 0)
    for h in range(2):
        everywhere("first_done", h)
        everywhere("spread", h, 3)
    used(2, 0)
    for i in range(4):
        if i > 0:
            for h in range(2):
                everywhere("pass_on", h, i)
        used(order[i], -1)
        used(order[i], 1)

    @pl.when(opening)
    def _():
        for h in range(2):
            for i in range(4):
                for j in range(4):
                    if i + j > 0:
                        come_back(h, i, j).wait_recv()
            go_over(h).wait_send()

    @pl.when(seg == 0)
    def _():
        for h in range(2):
            for m in range(micro):
                acc[m, :, h * half + most : (h + 1) * half] = dot(hbuf[m], wbuf[h, :, most:])

    for i in range(4):
        for h in range(2):
            everywhere("second_done", h, i)
            used(order[i], 2, (h,))

    @pl.when(seg == 0)
    def _():
        each_micro(lambda m: finish(m, "early"))

    everywhere("sent")

    @pl.when(closing)
    def _():
        visit.sent()
        for h in range(2):
            for i in range(4):
                for j in range(4):
                    if i + j > 0:
                        come_back(h, i, j).wait_send()

    def normed(m):
        def body(q, c):
            h = xbuf[m, :, chunk(q)].astype(F32) * invbuf[m] * gain[:, chunk(q)]
            hbuf[m, :, chunk(q)] = h.astype(BF16)
            return c

        over_chunks(body)

    def adapter_grads(m):
        glow = glowbuf[m]

        def body(q, c):
            seq[m, :, chunk(q)] = dot(glow, hbuf[m, :, chunk(q)], ((0,), (0,)))
            seq[micro + m, :, chunk(q)] = dot(lowbuf[m], gbuf[m, :, chunk(q)], ((0,), (0,)))
            return c

        over_chunks(body)

    def share_all():
        lax.fori_loop(1, members, share_start, 0)

    def backward(m, kind, between=None):
        if kind == "comes":
            acc[m] = jnp.zeros((rows, width), F32)

        size = 1 if kind == "comes" else 2

        def take_in(q, c):
            along, gl = c
            if kind != "rows":
                back(m, q, size).wait_recv()
            cols = columns_of(q, size)
            g = gbuf[m, :, cols]
            if kind == "comes":
                for i in range(2):
                    acc[m, :, i * half : (i + 1) * half] += dot(g, wbuf[i, cols, :])
            change = obuf[m, :, cols].astype(F32) - xbuf[m, :, cols].astype(F32)
            along = along + jnp.sum(g.astype(F32) * change, axis=1, keepdims=True)
            if kind == "rows":
                return along, gl
            return along, gl + dot(g, up[m, :, cols], ((1,), (1,)))

        along, gl = lax.fori_loop(0, CHUNKS // size, take_in, (column, narrow))
        if kind != "rows":
            glowbuf[m] = gl.astype(BF16)
        glow = glowbuf[m]
        inv = invbuf[m]
        coef = along / width * inv * inv
        if between is not None:
            between(m)
        at_once = 1 if kind == "columns" else 2

        def give_out(q, c):
            cols = columns_of(q, at_once)
            if kind == "comes":
                dh = acc[m, :, cols]
            elif kind in ("columns", "wide"):
                dh = dot(gbuf[m], by_columns(q, at_once))
            else:
                turned = dot(wbuf[0, cols, :], gbuf[m, :, :half], ((1,), (1,)))
                turned = turned + dot(wbuf[1, cols, :], gbuf[m, :, half:], ((1,), (1,)))
                dh = turned.T
            dh = dh + dot(glow, down[m, :, cols])
            out = gbuf[m, :, cols].astype(F32) + inv * (gain[:, cols] * dh)
            gout[m, :, cols] = (out - xbuf[m, :, cols].astype(F32) * coef).astype(BF16)

            if kind != "wide":
                back(m, q, at_once).start()
            return c

        lax.fori_loop(0, CHUNKS // at_once, give_out, 0)
        pltpu.make_async_copy(gout.at[m], grads_in.at[m], store_sem.at[micro + m]).start()

    even = lax.rem(seg, 2) == 0

    @pl.when(even & (seg > 0))
    def _():
        each_micro(lambda m: forward(m, "comes"))

    @pl.when(jnp.logical_not(even) & (seg < last))
    def _():
        each_micro(lambda m: forward(m, "columns"))

    @pl.when(seg < last)
    def _():
        each_micro(normed)

        size = 512
        count = width // size

        def place(i, j):
            inner = lax.rem(j, count // 2)
            return wbuf.at[
                j // (count // 2), pl.ds(pl.multiple_of(i * size, size), size), pl.ds(pl.multiple_of(inner * size, size), size)
            ]

        def turn(i, c):
            def inner(j, c):
                a, b = place(i, j)[...].T, place(j, i)[...].T
                place(j, i)[...] = a
                place(i, j)[...] = b
                return c

            return lax.fori_loop(i, count, inner, c)

        lax.fori_loop(0, count, turn, 0)

    def before_the_last(m):
        adapter_grads(m)

        @pl.when(m == micro - 1)
        def _():
            share_all()

    def and_grads(m, kind):
        backward(m, kind)
        adapter_grads(m)

    @pl.when(seg == 0)
    def _():
        each_micro(lambda m: backward(m, "wide", before_the_last))

    @pl.when(even & (seg > 0))
    def _():
        each_micro(lambda m: and_grads(m, "columns"))

    @pl.when(jnp.logical_not(even) & (seg < last))
    def _():
        each_micro(lambda m: and_grads(m, "comes"))

    @pl.when(seg == last)
    def _():
        pltpu.make_async_copy(cot, gbuf, load_sem.at[1]).wait()

        def ready(m):
            keep = lax.broadcasted_iota(jnp.int32, (rows, wide), 0) < lens[m, me]

            def masked(q, c):
                gbuf[m, :, chunk(q)] = jnp.where(keep, gbuf[m, :, chunk(q)].astype(F32), 0.0).astype(BF16)
                return c

            over_chunks(masked)
            glowbuf[m] = dot(gbuf[m], up[m], ((1,), (1,))).astype(BF16)

        def both(m):
            forward(m, "wide")
            backward(m, "rows")

        each_micro(ready)
        each_micro(both)
        each_micro(normed)
        each_micro(adapter_grads)

    @pl.when(seg > 0)
    def _():
        share_all()

    def add(mine, source, fresh):
        for t, target in enumerate((gdown, gup)):
            for s in range(skills):
                p = sum(mixb[s, pl.ds(m * members + source, 1), :] * mine[t * micro + m] for m in range(micro))
                p = p.astype(BF16).astype(F32)
                target[s] = p if fresh else target[s] + p

    own_cols = pl.ds(pl.multiple_of(me * block, block), block)
    add([seq[i, :, own_cols] for i in range(2 * micro)], me, True)

    def take(d, c):
        share(d).wait_recv()
        add([got[d, i] for i in range(2 * micro)], lax.rem(me - d + members, members), False)
        return c

    lax.fori_loop(1, members, take, 0)

    def drain(d, c):
        share(d).wait_send()
        return c

    lax.fori_loop(1, members, drain, 0)
    for m in range(micro):
        pltpu.make_async_copy(obuf.at[m], hidden.at[m], store_sem.at[m]).wait()
        pltpu.make_async_copy(gout.at[m], grads_in.at[m], store_sem.at[micro + m]).wait()

    def all_sent(copy, size):
        for m in range(micro):
            for q in range(CHUNKS // size):
                copy(m, q, size).wait_send()

    @pl.when(even)
    def _():
        all_sent(onward, 2)

    @pl.when(even & (seg > 0))
    def _():
        all_sent(back, 1)

    @pl.when(jnp.logical_not(even))
    def _():
        all_sent(back, 2)

    @pl.when(jnp.logical_not(even) & (seg < last))
    def _():
        all_sent(onward, 1)


def shards(embeds, base_weight, norm_gain, skill_down, skill_up, task_ids, allocation, target_lengths, cotangent):
    micro, _, rows, width = embeds.shape
    block = base_weight.shape[1]
    _, skills, rank, _ = skill_down.shape
    members = lax.axis_size("dp")
    anywhere = pl.BlockSpec(memory_space=pl.ANY)
    vmem = pl.BlockSpec(memory_space=pltpu.VMEM)
    smem = pl.BlockSpec(memory_space=pltpu.SMEM)
    stream = jax.ShapeDtypeStruct((micro, rows, width), BF16)
    grad = jax.ShapeDtypeStruct((skills, rank, block), F32)
    dma = pltpu.SemaphoreType.DMA
    held = pltpu.VMEM((micro, rows, width), BF16)
    hidden, grads_in, gdown, gup = pl.pallas_call(
        kernel,
        out_shape=(stream, stream, grad, grad),
        in_specs=[anywhere, anywhere, vmem, vmem, vmem, vmem, anywhere, smem, anywhere],
        out_specs=(anywhere, anywhere, vmem, vmem),
        scratch_shapes=[
            pltpu.VMEM((2, width, width // 2), BF16),
            pltpu.VMEM((2, width, width // 16), BF16),
            held, held, held, held, held,
            pltpu.VMEM((micro, rank, width), BF16),
            pltpu.VMEM((micro, rank, width), BF16),
            pltpu.VMEM((micro, rows, rank), BF16),
            pltpu.VMEM((micro, rows, rank), BF16),
            pltpu.VMEM((micro, rows, 1), F32),
            pltpu.VMEM((skills, micro * members, block), F32),
            pltpu.VMEM(allocation.shape[::-1], jnp.int32),
            pltpu.VMEM((micro, rows, width), F32),
            pltpu.VMEM((2 * micro, rank, width), F32),
            pltpu.VMEM((members, 2 * micro, rank, block), F32),
            *((dma((2, 4)), dma((2, 4)), dma((2, 4, 4)), dma((2, 4, 4))) * 3),
            dma((2,)), dma((2,)), dma((2, 16)), dma((2, 16)), dma((2,)),
            dma((micro, CHUNKS)), dma((micro, CHUNKS)), dma((micro, CHUNKS)), dma((micro, CHUNKS)),
            dma((3,)), dma((2 * micro,)), dma((members,)), dma((members,)), pltpu.SemaphoreType.REGULAR,
        ],
        compiler_params=pltpu.CompilerParams(
            collective_id=0, has_side_effects=True, vmem_limit_bytes=60 * 1024 * 1024
        ),
    )(
        embeds[:, 0], base_weight[0], norm_gain, skill_down[0], skill_up[0],
        task_ids, allocation.T, target_lengths, cotangent[:, 0],
    )
    return (hidden[None, :, None], grads_in[None, :, None], gdown[None], gup[None])


def solution(mesh):
    in_specs = (
        P(None, "dp", None, None),
        P("segment", "dp", None),
        P("segment", None),
        P("segment", None, None, None),
        P("segment", None, None, None),
        P(),
        P(),
        P(),
        P(None, "dp", None, None),
    )
    out_specs = (
        P("segment", None, "dp", None, None),
        P("segment", None, "dp", None, None),
        P("segment", None, None, "dp"),
        P("segment", None, None, "dp"),
    )
    return jax.shard_map(shards, mesh=mesh, in_specs=in_specs, out_specs=out_specs, check_vma=False)
```

```python
import functools

import jax
import jax.numpy as jnp
from jax import lax
from jax.experimental import pallas as pl
from jax.experimental.pallas import tpu as pltpu
from jax.sharding import PartitionSpec as P

EPS = 1e-06
MESH = pl.DeviceIdType.MESH
SIDE = 4
CHUNKS = 8
F32 = jnp.float32
BF16 = jnp.bfloat16


def dot(a, b, dims=((1,), (0,))):
    return lax.dot_general(a, b, (dims, ((), ())), preferred_element_type=F32)


def kernel(
    emb, w, gain, sdown, sup, tasks, alloc, lens, cot,
    hidden, grads_in, gdown, gup,
    wbuf, vis, xbuf, obuf, hbuf, gbuf, gout, down, up, lowbuf, glowbuf, invbuf, mixb, table, acc, seq, got,
    *sems,
):
    main_sems, rest_sems, visit_sems = sems[:4], sems[4:8], sems[8:12]
    over_s, over_r, back_s, back_r, own_sem = sems[12:17]
    x_s, x_r, g_s, g_r, load_sem, store_sem, seq_s, seq_r, turn_sem = sems[17:]
    segments = lax.axis_size("segment")
    members = lax.axis_size("dp")
    seg = lax.axis_index("segment")
    me = lax.axis_index("dp")
    micro, rows, width = emb.shape
    block = w.shape[0]
    half = width // 2
    part = block // 2
    skills, rank = sdown.shape[0], sdown.shape[1]
    z, y = me // SIDE, lax.rem(me, SIDE)
    last = segments - 1

    barrier = pltpu.get_barrier_semaphore()

    def greet(d, c):
        pl.semaphore_signal(barrier, inc=1, device_id=(seg, lax.rem(me + d, members)), device_id_type=MESH)
        return c

    lax.fori_loop(1, members, greet, 0)
    for d in (1, 2, segments - 2, segments - 1):
        pl.semaphore_signal(barrier, inc=1, device_id=(lax.rem(seg + d, segments), me), device_id_type=MESH)
    pl.semaphore_wait(barrier, members + 3)

    wide = width // CHUNKS

    def chunk(q):
        return pl.ds(pl.multiple_of(q * wide, wide), wide)

    def columns_of(q, at_once):
        size = at_once * wide
        return pl.ds(pl.multiple_of(q * size, size), size)

    def by_columns(q, at_once=1):
        count = half // (at_once * wide)
        return wbuf[q // count, :, columns_of(lax.rem(q, count), at_once)]

    def last_of(buf, m, q, at_once):
        count = half // (at_once * wide)
        final = pl.ds(width - wide, wide)
        return dot(buf[m, :, final], wbuf[q // count, final, columns_of(lax.rem(q, count), at_once)])

    def hop(buf, target, m, q, size, s, r, to):
        cols = columns_of(q, size)
        return pltpu.make_async_remote_copy(
            src_ref=buf.at[m, :, cols], dst_ref=target.at[m, :, cols], send_sem=s.at[m, q], recv_sem=r.at[m, q],
            device_id=(to, me), device_id_type=MESH,
        )

    onward = functools.partial(hop, obuf, xbuf, s=x_s, r=x_r, to=lax.rem(seg + 1, segments))
    back = functools.partial(hop, gout, gbuf, s=g_s, r=g_r, to=lax.rem(seg + last, segments))
    column = jnp.zeros((rows, 1), F32)
    narrow = jnp.zeros((rows, rank), F32)

    def share(d):
        to = lax.rem(me + d, members)
        return pltpu.make_async_remote_copy(
            src_ref=seq.at[:, :, pl.ds(pl.multiple_of(to * block, block), block)], dst_ref=got.at[d],
            send_sem=seq_s.at[d], recv_sem=seq_r.at[d], device_id=(seg, to), device_id_type=MESH,
        )

    def share_start(d, c):
        share(d).start()
        return c

    def over_chunks(body, init=0):
        return lax.fori_loop(0, CHUNKS, body, init)

    def each_micro(body):
        def step(m, c):
            body(m)
            return c

        lax.fori_loop(0, micro, step, 0)

    def begin(m, kind):
        if kind == "comes":
            acc[m] = jnp.zeros((rows, width), F32)

        size = 2 if kind in ("columns", "wide") else 1

        def take_in(q, c):
            ss, lw = c
            if kind != "early":
                onward(m, q, size).wait_recv()
            cols = columns_of(q, size)
            v = xbuf[m, :, cols].astype(F32)
            h = (v * gain[:, cols]).astype(BF16)
            hbuf[m, :, cols] = h
            if kind == "comes":

                @pl.when(q < CHUNKS - 1)
                def _():
                    for i in range(2):
                        acc[m, :, i * half : (i + 1) * half] += dot(h, wbuf[i, cols, :])

            return ss + jnp.sum(v * v, axis=1, keepdims=True), lw + dot(h, down[m, :, cols], ((1,), (1,)))

        ss, lw = lax.fori_loop(0, CHUNKS // size, take_in, (column, narrow))
        inv = lax.rsqrt(ss / width + EPS)
        invbuf[m] = inv
        lowbuf[m] = (lw * inv).astype(BF16)

    def finish(m, kind):
        inv = invbuf[m]
        low = lowbuf[m]

        at_once = {"columns": 1, "wide": 4}.get(kind, 2)

        def give_out(q, c):
            cols = columns_of(q, at_once)
            total = dot(hbuf[m], by_columns(q, at_once)) if kind in ("columns", "wide") else acc[m, :, cols]
            if kind == "comes":
                total = total + last_of(hbuf, m, q, at_once)
            total = xbuf[m, :, cols].astype(F32) + inv * total + dot(low, up[m, :, cols])
            obuf[m, :, cols] = total.astype(BF16)
            if kind != "wide":
                onward(m, q, at_once).start()
            return c

        lax.fori_loop(0, CHUNKS // at_once, give_out, 0)
        pltpu.make_async_copy(obuf.at[m], hidden.at[m], store_sem.at[m]).start()

    def forward(m, kind):
        begin(m, kind)
        finish(m, kind)

    extra = vis.shape[2]
    most = half - extra
    order = (0, -1, 1, 2)
    ways = (1, -1)
    opening = seg < 2
    closing = seg >= segments - 2

    def at(h, df, ds):
        dy, dz = (df, ds) if h == 0 else (ds, df)
        return lax.rem(z + dz + SIDE, SIDE) * SIDE + lax.rem(y + dy + SIDE, SIDE)

    def block_of(buf, cols, h, df, ds, sub=None):
        start = at(h, df, ds) * block
        if sub is None:
            return buf.at[h, pl.ds(pl.multiple_of(start, block), block), cols]
        return buf.at[h, pl.ds(pl.multiple_of(start + sub * part, part), part), cols]

    def remote(src, dst, s, r, to, to_seg=seg):
        return pltpu.make_async_remote_copy(
            src_ref=src, dst_ref=dst, send_sem=s, recv_sem=r, device_id=(to_seg, to), device_id_type=MESH
        )

    class Stream:
        def __init__(self, buf, cols, mine, f_s, f_r, s_s, s_r):
            self.ref = functools.partial(block_of, buf, cols)
            self.mine, self.sems = mine, (f_s, f_r, s_s, s_r)

        def first(self, h, d):
            way = ways[d % 2]
            dst = self.ref(h, 0, 0) if d < 2 else self.ref(h, -way, 0, d - 2)
            src = self.mine(h) if d < 2 else dst
            return remote(src, dst, self.sems[0].at[h, d], self.sems[1].at[h, d], at(h, way, 0))

        def second(self, h, i, d):
            way = ways[d % 2]
            dst = self.ref(h, order[i], 0) if d < 2 else self.ref(h, order[i], -way, d - 2)
            src = self.mine(h) if d < 2 and i == 0 else dst
            return remote(src, dst, self.sems[2].at[h, i, d], self.sems[3].at[h, i, d], at(h, 0, way))

        def open(self):
            for h in range(2):
                for d in range(2):
                    self.first(h, d).start()
            for h in range(2):
                self.spread(h, 0)

        def arrived_first(self, h):
            for d in range(2):
                self.first(h, d).wait_recv()
                self.first(h, 2 + d).start()

        def spread(self, h, i):
            for d in range(2):
                self.second(h, i, d).start()

        def pass_on(self, h, i):
            for d in range(2):
                self.second(h, i, d).wait_recv()
                self.second(h, i, 2 + d).start()

        def first_done(self, h):
            for d in range(2):
                self.first(h, 2 + d).wait_recv()

        def second_done(self, h, i):
            for d in range(2):
                self.second(h, i, 2 + d).wait_recv()

        def sent(self):
            for h in range(2):
                for d in range(4):
                    self.first(h, d).wait_send()
                    for i in range(4):
                        self.second(h, i, d).wait_send()

    side = pl.ds(most, extra)
    main = Stream(wbuf, pl.ds(0, most), lambda h: w.at[:, pl.ds(h * half, most)], *main_sems)
    rest = Stream(wbuf, side, lambda h: w.at[:, pl.ds(h * half + most, extra)], *rest_sems)
    visit = Stream(vis, pl.ds(0, extra), lambda h: block_of(vis, pl.ds(0, extra), h, 0, 0), *visit_sems)

    def go_over(h):
        return remote(
            w.at[:, pl.ds(h * half + most, extra)], block_of(vis, pl.ds(0, extra), h, 0, 0),
            over_s.at[h], over_r.at[h], me, lax.rem(seg + segments - 2, segments),
        )

    def come_back(h, i, j):
        return remote(
            block_of(vis, pl.ds(0, extra), h, order[i], order[j]), block_of(wbuf, side, h, order[i], order[j]),
            back_s.at[h, i * 4 + j], back_r.at[h, i * 4 + j], me, lax.rem(seg + 2, segments),
        )

    def on_all_but_opening(body):
        pl.when(jnp.logical_not(opening))(body)

    def start_own():
        main.open()
        on_all_but_opening(rest.open)

    @pl.when(opening)
    def _():
        for h in range(2):
            go_over(h).start()

    shared = seg >= 2
    later = shared & (lax.rem(seg, 2) == 1)

    @pl.when(jnp.logical_not(closing) & jnp.logical_not(later))
    def _():
        start_own()

    own = []
    for h in range(2):
        c = pltpu.make_async_copy(
            w.at[:, h * half : (h + 1) * half], block_of(wbuf, pl.ds(0, half), h, 0, 0), own_sem.at[h]
        )
        c.start()
        own.append(c)
    pltpu.make_async_copy(alloc, table, load_sem.at[2]).start()

    @pl.when(seg == 0)
    def _():
        pltpu.make_async_copy(emb, xbuf, load_sem.at[0]).start()

    @pl.when(seg == last)
    def _():
        pltpu.make_async_copy(cot, gbuf, load_sem.at[1]).start()


    @pl.when(closing)
    def _():
        for h in range(2):
            go_over(h).wait_recv()
        visit.open()
        pl.when(jnp.logical_not(later))(start_own)
        for h in range(2):
            visit.arrived_first(h)
        for h in range(2):
            visit.spread(h, 1)
            visit.spread(h, 2)
        for h in range(2):
            come_back(h, 1, 0).start()
            come_back(h, 2, 0).start()
            visit.pass_on(h, 0)
        for h in range(2):
            visit.first_done(h)
            visit.spread(h, 3)
        for i in range(4):
            for h in range(2):
                if i > 0:
                    visit.pass_on(h, i)
                come_back(h, i, 1).start()
                come_back(h, i, 2).start()
        for h in range(2):
            come_back(h, 3, 0).start()
        for i in range(4):
            for h in range(2):
                visit.second_done(h, i)
                come_back(h, i, 3).start()

    def everywhere(step, *which):
        getattr(main, step)(*which)
        on_all_but_opening(lambda: getattr(rest, step)(*which))

    @pl.when(jnp.logical_not(later))
    def _():
        for h in range(2):
            everywhere("arrived_first", h)

    @pl.when(shared & jnp.logical_not(later))
    def _():
        pl.semaphore_signal(turn_sem, inc=1, device_id=(lax.rem(seg + 1, segments), me), device_id_type=MESH)

    pltpu.make_async_copy(alloc, table, load_sem.at[2]).wait()
    known = table[...].astype(F32).astype(BF16)
    for m in range(micro):
        picked = lax.broadcasted_iota(jnp.int32, (table.shape[1], members), 0) == tasks[m : m + 1, :]
        uses = dot(picked.astype(F32).astype(BF16), known, ((0,), (1,)))
        mix = uses / jnp.maximum(jnp.sum(uses, axis=1, keepdims=True), 1.0)
        for s in range(skills):
            mixb[s, m * members : (m + 1) * members] = jnp.broadcast_to(mix[:, s : s + 1], (members, mixb.shape[2]))
    step = mixb.shape[2]

    def adapters(i, c):
        cols = pl.ds(pl.multiple_of(i * step, step), step)
        for m in range(micro):
            for source, target in ((sdown, down), (sup, up)):
                acc = jnp.zeros((rank, step), F32)
                for s in range(skills):
                    acc = acc + mixb[s, pl.ds(m * members + me, 1), :] * source[s, :, cols].astype(F32)
                target[m, :, cols] = acc.astype(BF16)
        return c

    lax.fori_loop(0, width // step, adapters, 0)

    @pl.when(later)
    def _():
        pl.semaphore_wait(turn_sem, 1)
        start_own()
        for h in range(2):
            everywhere("arrived_first", h)

    @pl.when(seg == 0)
    def _():
        pltpu.make_async_copy(emb, xbuf, load_sem.at[0]).wait()
        each_micro(lambda m: begin(m, "early"))
        acc[...] = jnp.zeros_like(acc)

    def used(df, ds, hs=(0, 1)):
        @pl.when(seg == 0)
        def _():
            for h in hs:
                start = pl.multiple_of(at(h, df, ds) * block, block)
                for m in range(micro):
                    acc[m, :, h * half : h * half + most] += dot(
                        hbuf[m, :, pl.ds(start, block)], wbuf[h, pl.ds(start, block), :most]
                    )

    for h in range(2):
        everywhere("spread", h, 1)
        everywhere("spread", h, 2)
    for h in range(2):
        own[h].wait()
    used(0, 0)
    used(-1, 0)
    used(1, 0)
    for h in range(2):
        everywhere("pass_on", h, 0)
    for h in range(2):
        everywhere("first_done", h)
        everywhere("spread", h, 3)
    used(2, 0)
    for i in range(4):
        if i > 0:
            for h in range(2):
                everywhere("pass_on", h, i)
        used(order[i], -1)
        used(order[i], 1)

    @pl.when(opening)
    def _():
        for h in range(2):
            for i in range(4):
                for j in range(4):
                    if i + j > 0:
                        come_back(h, i, j).wait_recv()
            go_over(h).wait_send()

    @pl.when(seg == 0)
    def _():
        for h in range(2):
            for m in range(micro):
                acc[m, :, h * half + most : (h + 1) * half] = dot(hbuf[m], wbuf[h, :, most:])

    for i in range(4):
        for h in range(2):
            everywhere("second_done", h, i)
            used(order[i], 2, (h,))

    @pl.when(seg == 0)
    def _():
        each_micro(lambda m: finish(m, "early"))

    everywhere("sent")

    @pl.when(closing)
    def _():
        visit.sent()
        for h in range(2):
            for i in range(4):
                for j in range(4):
                    if i + j > 0:
                        come_back(h, i, j).wait_send()

    def normed(m):
        def body(q, c):
            h = xbuf[m, :, chunk(q)].astype(F32) * invbuf[m] * gain[:, chunk(q)]
            hbuf[m, :, chunk(q)] = h.astype(BF16)
            return c

        over_chunks(body)

    def adapter_grads(m):
        glow = glowbuf[m]

        def body(q, c):
            seq[m, :, chunk(q)] = dot(glow, hbuf[m, :, chunk(q)], ((0,), (0,)))
            seq[micro + m, :, chunk(q)] = dot(lowbuf[m], gbuf[m, :, chunk(q)], ((0,), (0,)))
            return c

        over_chunks(body)

    def share_all():
        lax.fori_loop(1, members, share_start, 0)

    def backward(m, kind, between=None):
        if kind == "comes":
            acc[m] = jnp.zeros((rows, width), F32)

        size = 1 if kind == "comes" else 2

        def take_in(q, c):
            along, gl = c
            if kind != "rows":
                back(m, q, size).wait_recv()
            cols = columns_of(q, size)
            g = gbuf[m, :, cols]
            if kind == "comes":

                @pl.when(q < CHUNKS - 1)
                def _():
                    for i in range(2):
                        acc[m, :, i * half : (i + 1) * half] += dot(g, wbuf[i, cols, :])

            change = obuf[m, :, cols].astype(F32) - xbuf[m, :, cols].astype(F32)
            along = along + jnp.sum(g.astype(F32) * change, axis=1, keepdims=True)
            if kind == "rows":
                return along, gl
            return along, gl + dot(g, up[m, :, cols], ((1,), (1,)))

        along, gl = lax.fori_loop(0, CHUNKS // size, take_in, (column, narrow))
        if kind != "rows":
            glowbuf[m] = gl.astype(BF16)
        glow = glowbuf[m]
        inv = invbuf[m]
        coef = along / width * inv * inv
        if between is not None:
            between(m)
        at_once = {"columns": 1, "wide": 4}.get(kind, 2)

        def give_out(q, c):
            cols = columns_of(q, at_once)
            if kind == "comes":
                dh = acc[m, :, cols] + last_of(gbuf, m, q, at_once)
            elif kind in ("columns", "wide"):
                dh = dot(gbuf[m], by_columns(q, at_once))
            else:
                turned = dot(wbuf[0, cols, :], gbuf[m, :, :half], ((1,), (1,)))
                turned = turned + dot(wbuf[1, cols, :], gbuf[m, :, half:], ((1,), (1,)))
                dh = turned.T
            dh = dh + dot(glow, down[m, :, cols])
            out = gbuf[m, :, cols].astype(F32) + inv * (gain[:, cols] * dh)
            gout[m, :, cols] = (out - xbuf[m, :, cols].astype(F32) * coef).astype(BF16)

            if kind != "wide":
                back(m, q, at_once).start()
            return c

        lax.fori_loop(0, CHUNKS // at_once, give_out, 0)
        pltpu.make_async_copy(gout.at[m], grads_in.at[m], store_sem.at[micro + m]).start()

    even = lax.rem(seg, 2) == 0

    @pl.when(even & (seg > 0))
    def _():
        each_micro(lambda m: forward(m, "comes"))

    @pl.when(jnp.logical_not(even) & (seg < last))
    def _():
        each_micro(lambda m: forward(m, "columns"))

    @pl.when(seg < last)
    def _():
        each_micro(normed)

        size = 512
        count = width // size

        def place(i, j):
            inner = lax.rem(j, count // 2)
            return wbuf.at[
                j // (count // 2), pl.ds(pl.multiple_of(i * size, size), size), pl.ds(pl.multiple_of(inner * size, size), size)
            ]

        def turn(i, c):
            def inner(j, c):
                a, b = place(i, j)[...].T, place(j, i)[...].T
                place(j, i)[...] = a
                place(i, j)[...] = b
                return c

            return lax.fori_loop(i, count, inner, c)

        lax.fori_loop(0, count, turn, 0)

    def before_the_last(m):
        adapter_grads(m)

        @pl.when(m == micro - 1)
        def _():
            share_all()

    def and_grads(m, kind):
        backward(m, kind)
        adapter_grads(m)

    @pl.when(seg == 0)
    def _():
        each_micro(lambda m: backward(m, "wide", before_the_last))

    @pl.when(even & (seg > 0))
    def _():
        each_micro(lambda m: and_grads(m, "columns"))

    @pl.when(jnp.logical_not(even) & (seg < last))
    def _():
        each_micro(lambda m: and_grads(m, "comes"))

    @pl.when(seg == last)
    def _():
        pltpu.make_async_copy(cot, gbuf, load_sem.at[1]).wait()

        def ready(m):
            keep = lax.broadcasted_iota(jnp.int32, (rows, wide), 0) < lens[m, me]

            def masked(q, c):
                gbuf[m, :, chunk(q)] = jnp.where(keep, gbuf[m, :, chunk(q)].astype(F32), 0.0).astype(BF16)
                return c

            over_chunks(masked)
            glowbuf[m] = dot(gbuf[m], up[m], ((1,), (1,))).astype(BF16)

        def both(m):
            forward(m, "wide")
            backward(m, "rows")

        each_micro(ready)
        each_micro(both)
        each_micro(normed)
        each_micro(adapter_grads)

    @pl.when(seg > 0)
    def _():
        share_all()

    def add(mine, source, fresh):
        for t, target in enumerate((gdown, gup)):
            for s in range(skills):
                p = sum(mixb[s, pl.ds(m * members + source, 1), :] * mine[t * micro + m] for m in range(micro))
                p = p.astype(BF16).astype(F32)
                target[s] = p if fresh else target[s] + p

    own_cols = pl.ds(pl.multiple_of(me * block, block), block)
    add([seq[i, :, own_cols] for i in range(2 * micro)], me, True)

    def take(d, c):
        share(d).wait_recv()
        add([got[d, i] for i in range(2 * micro)], lax.rem(me - d + members, members), False)
        return c

    lax.fori_loop(1, members, take, 0)

    def drain(d, c):
        share(d).wait_send()
        return c

    lax.fori_loop(1, members, drain, 0)
    for m in range(micro):
        pltpu.make_async_copy(obuf.at[m], hidden.at[m], store_sem.at[m]).wait()
        pltpu.make_async_copy(gout.at[m], grads_in.at[m], store_sem.at[micro + m]).wait()

    def all_sent(copy, size):
        for m in range(micro):
            for q in range(CHUNKS // size):
                copy(m, q, size).wait_send()

    @pl.when(even)
    def _():
        all_sent(onward, 2)

    @pl.when(even & (seg > 0))
    def _():
        all_sent(back, 1)

    @pl.when(jnp.logical_not(even))
    def _():
        all_sent(back, 2)

    @pl.when(jnp.logical_not(even) & (seg < last))
    def _():
        all_sent(onward, 1)


def shards(embeds, base_weight, norm_gain, skill_down, skill_up, task_ids, allocation, target_lengths, cotangent):
    micro, _, rows, width = embeds.shape
    block = base_weight.shape[1]
    _, skills, rank, _ = skill_down.shape
    members = lax.axis_size("dp")
    anywhere = pl.BlockSpec(memory_space=pl.ANY)
    vmem = pl.BlockSpec(memory_space=pltpu.VMEM)
    smem = pl.BlockSpec(memory_space=pltpu.SMEM)
    stream = jax.ShapeDtypeStruct((micro, rows, width), BF16)
    grad = jax.ShapeDtypeStruct((skills, rank, block), F32)
    dma = pltpu.SemaphoreType.DMA
    held = pltpu.VMEM((micro, rows, width), BF16)
    hidden, grads_in, gdown, gup = pl.pallas_call(
        kernel,
        out_shape=(stream, stream, grad, grad),
        in_specs=[anywhere, anywhere, vmem, vmem, vmem, vmem, anywhere, smem, anywhere],
        out_specs=(anywhere, anywhere, vmem, vmem),
        scratch_shapes=[
            pltpu.VMEM((2, width, width // 2), BF16),
            pltpu.VMEM((2, width, width // 16), BF16),
            held, held, held, held, held,
            pltpu.VMEM((micro, rank, width), BF16),
            pltpu.VMEM((micro, rank, width), BF16),
            pltpu.VMEM((micro, rows, rank), BF16),
            pltpu.VMEM((micro, rows, rank), BF16),
            pltpu.VMEM((micro, rows, 1), F32),
            pltpu.VMEM((skills, micro * members, block), F32),
            pltpu.VMEM(allocation.shape[::-1], jnp.int32),
            pltpu.VMEM((micro, rows, width), F32),
            pltpu.VMEM((2 * micro, rank, width), F32),
            pltpu.VMEM((members, 2 * micro, rank, block), F32),
            *((dma((2, 4)), dma((2, 4)), dma((2, 4, 4)), dma((2, 4, 4))) * 3),
            dma((2,)), dma((2,)), dma((2, 16)), dma((2, 16)), dma((2,)),
            dma((micro, CHUNKS)), dma((micro, CHUNKS)), dma((micro, CHUNKS)), dma((micro, CHUNKS)),
            dma((3,)), dma((2 * micro,)), dma((members,)), dma((members,)), pltpu.SemaphoreType.REGULAR,
        ],
        compiler_params=pltpu.CompilerParams(
            collective_id=0, has_side_effects=True, vmem_limit_bytes=60 * 1024 * 1024
        ),
    )(
        embeds[:, 0], base_weight[0], norm_gain, skill_down[0], skill_up[0],
        task_ids, allocation.T, target_lengths, cotangent[:, 0],
    )
    return (hidden[None, :, None], grads_in[None, :, None], gdown[None], gup[None])


def solution(mesh):
    in_specs = (
        P(None, "dp", None, None),
        P("segment", "dp", None),
        P("segment", None),
        P("segment", None, None, None),
        P("segment", None, None, None),
        P(),
        P(),
        P(),
        P(None, "dp", None, None),
    )
    out_specs = (
        P("segment", None, "dp", None, None),
        P("segment", None, "dp", None, None),
        P("segment", None, None, "dp"),
        P("segment", None, None, "dp"),
    )
    return jax.shard_map(shards, mesh=mesh, in_specs=in_specs, out_specs=out_specs, check_vma=False)
```
